128 devices in a mesh: gx: 4 (over x), gy: 32 (over z, y, core).
Axes of the slice: x: 4, y: 4, z: 4, core: 2. Of those that a mesh axis runs over, the one named last changes fastest.
Arguments:
- positions: float32 [8192, 3, 128], P(('gx', 'gy')), may hold values from 0 to 64, as said below
- charges: float32 [8192, 128], P(('gx', 'gy')), may hold values from -8 to 8, as said below
- send_x: int32 [128, 2, 32], P(('gx', 'gy')), may hold values from -1 to 63, as said below
- send_y: int32 [128, 2, 32], P(('gx', 'gy')), may hold values from -1 to 63, as said below
- send_corner: int32 [128, 4, 16], P(('gx', 'gy')), may hold values from -1 to 63, as said below
- near_slot: int32 [8192, 27], P(('gx', 'gy')), may hold values from -1 to 255, as said below
- far_sources: int32 [1024, 316], P(('gx', 'gy')), may hold values from -1 to 1023, as said below
- translations: bfloat16 [121, 38236], replicated, may hold values from -0.0078125 to 0.0078125
Outputs:
- potential: float32 [8192, 128], P(('gx', 'gy'))
- field_strength: float32 [8192, 3, 128], P(('gx', 'gy'))
The draws below stay inside these ranges and needn't reach their ends.
Inputs may be any that keep to these rules, and one draw needn't show every extreme that they name: `send_x`: row [s, k] lists in increasing order, padded with -1, the local indices of the leaves of device s that hold particles and have local x coordinate 0 (k = 0) or 2 - 1 (k = 1); in every draw some device fills both rows. `send_y`: row [s, k] lists in increasing order, padded with -1, the local indices of the leaves of device s that hold particles and have local y coordinate 0 (k = 0) or 2 - 1 (k = 1); in every draw some device fills both rows. `send_corner`: row [s, k], k = 2 kx + ky, lists in increasing order, padded with -1, the local indices of the leaves of device s that hold particles and have local x coordinate kx (1) and local y coordinate ky (1); in every draw some device fills all four rows. `near_slot`: offset n = 9 (a + 1) + 3 (b + 1) + (c + 1) for the neighbour at (a, b, c) in -1..1; -1 where that leaf lies outside the domain or holds no particles; otherwise the entry of the owner's source table that holds it (n = 13 is the leaf itself). `far_sources`: class k is the k-th offset (a, b, c) in -3..3 with max(|a|, |b|, |c|) > 1, taken in increasing 49 a + 7 b + c; the entry is the upper cell at that offset where it lies in the domain, holds particles and its parent (coordinates halved, rounded down) touches or equals the parent of m, else -1. positions[g, :, p] lies in the unit box of leaf g. `charges`: empty leaves and the slots after each leaf's particle count hold zero.
All inputs are finite; a program needn't handle non-finite values.
Results may differ from the reference program's by a relative error of at most 0.0003.
Values may be sent and summed in bfloat16 or wider, within the bound.
A program may use at most 64 MiB of HBM per device.

```python
import math
import jax
import jax.numpy as jnp
import numpy as np
from jax import lax

ORDER = 10
COEF = 121
LEAF = 128
CLASSES = 316
BX = 2
BY = 2
BZ = 16
LEAF_DEV = 64
UP_DEV = 8
UP_CELLS = 1024
LEAVES = 8192
X_CELLS = 8
Y_CELLS = 64
CAP_X = 32
CAP_Y = 32
CAP_C = 16


near_offsets = [(first_a, first_b, first_c) for first_a in (-1, 0, 1) for first_b in (-1, 0, 1) for first_c in (-1, 0, 1)]


far_offsets = [(first_a, first_b, first_c) for first_a in range(-3, 4) for first_b in range(-3, 4) for first_c in range(-3, 4) if max(abs(first_a), abs(first_b), abs(first_c)) > 1]


def device_rows():
    return Y_CELLS // BY


def leaf_layout():
    local_ids = np.arange(LEAF_DEV)
    upper_ids = local_ids // 8
    half_y = BY // 2
    half_z = BZ // 2
    upper_x = upper_ids // (half_y * half_z)
    upper_y = upper_ids // half_z % half_y
    upper_z = upper_ids % half_z
    return (2 * upper_x + local_ids % 2, 2 * upper_y + local_ids // 2 % 2, 2 * upper_z + local_ids // 4 % 2)


def leaf_geometry():
    row_count = device_rows()
    device_count = LEAVES // LEAF_DEV
    local_x, local_y, local_z = leaf_layout()
    devices = np.arange(device_count)
    coord_x = ((devices // row_count)[:, None] * BX + local_x[None]).reshape(-1)
    coord_y = ((devices % row_count)[:, None] * BY + local_y[None]).reshape(-1)
    coord_z = np.tile(local_z, device_count)
    return (coord_x, coord_y, coord_z)


def leaf_index(coord_x, coord_y, coord_z):
    row_count = device_rows()
    device = coord_x // BX * row_count + coord_y // BY
    within_x = coord_x % BX
    within_y = coord_y % BY
    upper_ids = (within_x // 2 * (BY // 2) + within_y // 2) * (BZ // 2) + coord_z // 2
    return device * LEAF_DEV + 8 * upper_ids + within_x % 2 + 2 * (within_y % 2) + 4 * (coord_z % 2)


def occupancy(key):
    device_count = LEAVES // LEAF_DEV
    density = jax.random.randint(jax.random.fold_in(key, 11), (device_count,), 1, 9)
    density = density.at[device_rows() + 1].set(8)
    density = density.at[device_count - 1].set(8)
    throws = jax.random.randint(jax.random.fold_in(key, 12), (LEAVES,), 0, 8)
    owners = jnp.arange(LEAVES, dtype=jnp.int32) // LEAF_DEV
    return throws < density[owners]


def particle_live(key):
    occupied = occupancy(key)
    counts = jax.random.randint(jax.random.fold_in(key, 13), (LEAVES,), LEAF // 4, LEAF + 1)
    counts = counts.at[0].set(LEAF)
    counts = jnp.where(occupied, counts, 0)
    slot_index = jnp.arange(LEAF, dtype=jnp.int32)
    return slot_index[None, :] < counts[:, None]


def x_faces():
    local_x, local_y, local_z = leaf_layout()
    return np.stack([local_x == 0, local_x == BX - 1], axis=0)


def y_faces():
    local_x, local_y, local_z = leaf_layout()
    return np.stack([local_y == 0, local_y == BY - 1], axis=0)


def edge_faces():
    local_x, local_y, local_z = leaf_layout()
    rows_kept = []
    for kind in range(4):
        rows_kept.append((local_x == (BX - 1) * (kind // 2)) & (local_y == (BY - 1) * (kind % 2)))
    return np.stack(rows_kept, axis=0)


def face_lists(occupied, faces, capacity):
    device_count = LEAVES // LEAF_DEV
    kinds = faces.shape[0]
    held = occupied.reshape(device_count, 1, LEAF_DEV) & jnp.asarray(faces)[None]
    placed = jnp.cumsum(held.astype(jnp.int32), axis=2) - 1
    target = jnp.where(held, placed, capacity)
    shape = held.shape
    sender = jnp.broadcast_to(jnp.arange(device_count, dtype=jnp.int32)[:, None, None], shape)
    kind_ids = jnp.broadcast_to(jnp.arange(kinds, dtype=jnp.int32)[None, :, None], shape)
    leaf_ids = jnp.broadcast_to(jnp.arange(LEAF_DEV, dtype=jnp.int32)[None, None, :], shape)
    listing = jnp.full((device_count, kinds, capacity), -1, jnp.int32)
    listing = listing.at[sender, kind_ids, target].set(leaf_ids, mode='drop')
    return (listing, placed)


def draw_positions(key, part):
    coord_x, coord_y, coord_z = leaf_geometry()
    corner = jnp.asarray(np.stack([coord_x, coord_y, coord_z], axis=1).astype(np.float32))
    within_leaf = jax.random.uniform(jax.random.fold_in(key, 31), (LEAVES, 3, LEAF), jnp.float32)
    return corner[:, :, None] + within_leaf


def draw_charges(key, part):
    present = particle_live(key)
    sample = jax.random.normal(jax.random.fold_in(key, 21), (LEAVES, LEAF), jnp.float32)
    sample = jnp.clip(sample, -4.0, 4.0)
    return jnp.where(present, sample, 0.0)


def draw_send_x(key, part):
    return face_lists(occupancy(key), x_faces(), CAP_X)[0]


def draw_send_y(key, part):
    return face_lists(occupancy(key), y_faces(), CAP_Y)[0]


def draw_send_corner(key, part):
    return face_lists(occupancy(key), edge_faces(), CAP_C)[0]


def draw_near_slot(key, part):
    occupied = occupancy(key)
    placed_x = face_lists(occupied, x_faces(), CAP_X)[1]
    placed_y = face_lists(occupied, y_faces(), CAP_Y)[1]
    placed_edge = face_lists(occupied, edge_faces(), CAP_C)[1]
    coord_x, coord_y, coord_z = leaf_geometry()
    row_count = device_rows()
    own_device = np.arange(LEAVES) // LEAF_DEV
    columns = []
    for offset in near_offsets:
        moved_x = coord_x + offset[0]
        moved_y = coord_y + offset[1]
        moved_z = coord_z + offset[2]
        inside = (moved_x >= 0) & (moved_x < X_CELLS) & (moved_y >= 0) & (moved_y < Y_CELLS) & (moved_z >= 0) & (moved_z < BZ)
        target = leaf_index(np.clip(moved_x, 0, X_CELLS - 1), np.clip(moved_y, 0, Y_CELLS - 1), np.clip(moved_z, 0, BZ - 1))
        source_device = target // LEAF_DEV
        source_leaf = target % LEAF_DEV
        step_x = source_device // row_count - own_device // row_count
        step_y = source_device % row_count - own_device % row_count
        block_x = (step_x + 1) // 2
        block_y = (step_y + 1) // 2
        block_edge = 2 * block_x + block_y
        located_x = placed_x[source_device, np.clip(1 - block_x, 0, 1), source_leaf]
        located_y = placed_y[source_device, np.clip(1 - block_y, 0, 1), source_leaf]
        located_edge = placed_edge[source_device, np.clip(3 - block_edge, 0, 3), source_leaf]
        slot_x = LEAF_DEV + block_x * CAP_X + located_x
        slot_y = LEAF_DEV + 2 * CAP_X + block_y * CAP_Y + located_y
        slot_edge = LEAF_DEV + 2 * CAP_X + 2 * CAP_Y + block_edge * CAP_C + located_edge
        remote = jnp.where(step_y == 0, slot_x, jnp.where(step_x == 0, slot_y, slot_edge))
        same = (step_x == 0) & (step_y == 0)
        slot_ids = jnp.where(same, source_leaf, remote)
        present = inside & occupied[target]
        columns.append(jnp.where(present, slot_ids, -1))
    return jnp.stack(columns, axis=1).astype(jnp.int32)


def draw_far_sources(key, part):
    occupied = occupancy(key)
    filled = occupied.reshape(UP_CELLS, 8).any(axis=1)
    row_count = device_rows()
    device_count = LEAVES // LEAF_DEV
    half_x = BX // 2
    half_y = BY // 2
    half_z = BZ // 2
    upper_ids = np.arange(UP_DEV)
    devices = np.arange(device_count)
    cell_x = ((devices // row_count)[:, None] * half_x + (upper_ids // (half_y * half_z))[None]).reshape(-1)
    cell_y = ((devices % row_count)[:, None] * half_y + (upper_ids // half_z % half_y)[None]).reshape(-1)
    cell_z = np.tile(upper_ids % half_z, device_count)
    extent_x = X_CELLS // 2
    extent_y = Y_CELLS // 2
    columns = []
    for offset in far_offsets:
        moved_x = cell_x + offset[0]
        moved_y = cell_y + offset[1]
        moved_z = cell_z + offset[2]
        inside = (moved_x >= 0) & (moved_x < extent_x) & (moved_y >= 0) & (moved_y < extent_y) & (moved_z >= 0) & (moved_z < half_z)
        clip_x = np.clip(moved_x, 0, extent_x - 1)
        clip_y = np.clip(moved_y, 0, extent_y - 1)
        clip_z = np.clip(moved_z, 0, half_z - 1)
        parent_near = inside & (np.abs(clip_x // 2 - cell_x // 2) <= 1) & (np.abs(clip_y // 2 - cell_y // 2) <= 1) & (np.abs(clip_z // 2 - cell_z // 2) <= 1)
        device = clip_x // half_x * row_count + clip_y // half_y
        morton = device * UP_DEV + (clip_x % half_x * half_y + clip_y % half_y) * half_z + clip_z
        usable = parent_near & filled[morton]
        columns.append(jnp.where(usable, morton, -1))
    return jnp.stack(columns, axis=1).astype(jnp.int32)


def noise(own_key, shape, scale, limit, kind=jnp.bfloat16):
    values = scale * jax.random.normal(own_key, shape, jnp.float32)
    return jnp.clip(values, min=-limit, max=limit).astype(kind)


def setup_inputs(seed: int = 0) -> dict:
    streams_of = jax.random.split(jax.random.key(seed), 9)
    positions = draw_positions(jax.random.fold_in(streams_of[8], 71), 0)
    charges = draw_charges(jax.random.fold_in(streams_of[8], 71), 0)
    send_x = draw_send_x(jax.random.fold_in(streams_of[8], 71), 0)
    send_y = draw_send_y(jax.random.fold_in(streams_of[8], 71), 0)
    send_corner = draw_send_corner(jax.random.fold_in(streams_of[8], 71), 0)
    near_slot = draw_near_slot(jax.random.fold_in(streams_of[8], 71), 0)
    far_sources = draw_far_sources(jax.random.fold_in(streams_of[8], 71), 0)
    translations = noise(streams_of[7], (COEF, CLASSES * COEF), (16 * CLASSES * COEF) ** -0.5, 0.0078125)
    return {"positions": positions, "charges": charges, "send_x": send_x, "send_y": send_y, "send_corner": send_corner, "near_slot": near_slot, "far_sources": far_sources, "translations": translations}


softening = 0.01

def upper_centers(cells, row_count):
    half_y = BY // 2
    half_z = BZ // 2
    device = cells // UP_DEV
    local_ids = cells % UP_DEV
    cell_x = device // row_count * (BX // 2) + local_ids // (half_y * half_z)
    cell_y = device % row_count * half_y + local_ids // half_z % half_y
    cell_z = local_ids % half_z
    return 2.0 * jnp.stack([cell_x, cell_y, cell_z], axis=1).astype(jnp.float32) + 1.0

def harmonics(xcoord, ycoord, zcoord):
    radius_sq = xcoord * xcoord + ycoord * ycoord + zcoord * zcoord
    unity = jnp.ones_like(xcoord)
    nothing = jnp.zeros_like(xcoord)
    solid_harm = {(0, 0): (unity, nothing)}
    for moment in range(1, ORDER + 1):
        real_part, imag_part = solid_harm[moment - 1, moment - 1]
        factor = -0.5 / moment
        solid_harm[moment, moment] = (factor * (xcoord * real_part - ycoord * imag_part), factor * (xcoord * imag_part + ycoord * real_part))
    for moment in range(ORDER + 1):
        if moment + 1 <= ORDER:
            real_part, imag_part = solid_harm[moment, moment]
            solid_harm[moment + 1, moment] = (zcoord * real_part, zcoord * imag_part)
        for degree in range(moment + 2, ORDER + 1):
            factor = 1.0 / ((degree - moment) * (degree + moment))
            one_back = solid_harm[degree - 1, moment]
            two_back = solid_harm[degree - 2, moment]
            solid_harm[degree, moment] = (factor * ((2 * degree - 1) * zcoord * one_back[0] - radius_sq * two_back[0]), factor * ((2 * degree - 1) * zcoord * one_back[1] - radius_sq * two_back[1]))
    stacked = []
    for degree in range(ORDER + 1):
        for moment in range(degree + 1):
            scaling = math.sqrt(math.factorial(degree + moment) * math.factorial(degree - moment))
            real_part, imag_part = solid_harm[degree, moment]
            stacked.append(scaling * real_part)
            if moment > 0:
                stacked.append(scaling * imag_part)
    return jnp.stack(stacked, axis=0)

def leaf_multipoles(positions, charges, centers):
    repeated = jnp.repeat(centers, 8, axis=0)
    offsets = positions - repeated[:, :, None]
    harm = harmonics(offsets[:, 0], offsets[:, 1], offsets[:, 2])
    per_leaf = lax.optimization_barrier(jnp.sum(harm * charges[None], axis=2))
    return per_leaf.reshape(COEF, -1, 8).sum(axis=2)

def far_field(positions, centers, local_exp):
    repeated = jnp.repeat(centers, 8, axis=0)
    per_leaf = jnp.repeat(local_exp, 8, axis=1)

    def summed_field(points):
        offsets = points - repeated[:, :, None]
        harm = harmonics(offsets[:, 0], offsets[:, 1], offsets[:, 2])
        return lax.optimization_barrier(jnp.sum(harm * per_leaf[:, :, None], axis=0))
    potential, pullback = jax.vjp(summed_field, positions)
    gradient = pullback(jnp.ones_like(potential))[0]
    return (potential, -gradient)

def near_field(targets, source_points, source_charge, slot_ids):
    identity = jnp.eye(targets.shape[2], dtype=jnp.float32)

    def neighbour_step(running, inputs):
        potential, electric = running
        column, neighbour = inputs
        present = column >= 0
        safe = jnp.maximum(column, 0)
        points = source_points[safe]
        charge = jnp.where(present[:, None], source_charge[safe], 0.0)
        separation = targets[:, :, :, None] - points[:, :, None, :]
        distance = lax.optimization_barrier(jnp.sum(separation * separation, axis=1)) + softening
        inverse = lax.rsqrt(distance)
        self_mask = jnp.where(neighbour == 13, 1.0 - identity, 1.0)
        weight = charge[:, None, :] * inverse * self_mask
        potential = potential + lax.optimization_barrier(jnp.sum(weight, axis=2))
        electric = electric + lax.optimization_barrier(jnp.sum(separation * (weight * inverse * inverse)[:, None], axis=3))
        return ((potential, electric), None)
    start = (jnp.zeros(targets.shape[:1] + targets.shape[2:], jnp.float32), jnp.zeros(targets.shape, jnp.float32))
    result = lax.scan(neighbour_step, start, (slot_ids.T, jnp.arange(27, dtype=jnp.int32)))[0]
    return result

def source_blocks(send_x, send_y, send_corner):
    blocks = []
    for block in range(2):
        blocks.append((2 * block - 1, 0, send_x, 1 - block))
    for block in range(2):
        blocks.append((0, 2 * block - 1, send_y, 1 - block))
    for block in range(4):
        blocks.append((2 * (block // 2) - 1, 2 * (block % 2) - 1, send_corner, 3 - block))
    return blocks

def reference(positions, charges, send_x, send_y, send_corner, near_slot, far_sources, translations):
    row_count = Y_CELLS // BY
    column_count = X_CELLS // BX
    device_count = row_count * column_count
    upper_cells = jnp.arange(UP_CELLS, dtype=jnp.int32)
    centers = upper_centers(upper_cells, row_count)
    multipole = leaf_multipoles(positions, charges, centers).astype(jnp.bfloat16)
    usable = far_sources >= 0
    picked = jnp.take(multipole, jnp.maximum(far_sources, 0), axis=1)
    picked = jnp.where(usable[None], picked, jnp.zeros((), picked.dtype))
    stacked = jnp.transpose(picked, (1, 2, 0)).reshape(UP_CELLS, CLASSES * COEF)
    local_exp = jnp.einsum('uk,ik->iu', stacked.astype(jnp.float32), translations.astype(jnp.float32))
    far_pot, far_force = far_field(positions, centers, local_exp)
    blocks = source_blocks(send_x, send_y, send_corner)

    def per_device(device):
        grid_x = device // row_count
        grid_y = device % row_count
        table_parts = [device * LEAF_DEV + jnp.arange(LEAF_DEV, dtype=jnp.int32)]
        present_parts = [jnp.ones((LEAF_DEV,), jnp.bool_)]
        for step_x, step_y, listing, kind in blocks:
            peer_x = grid_x + step_x
            peer_y = grid_y + step_y
            valid = (peer_x >= 0) & (peer_x < column_count) & (peer_y >= 0) & (peer_y < row_count)
            peer = jnp.clip(peer_x, 0, column_count - 1) * row_count + jnp.clip(peer_y, 0, row_count - 1)
            incoming = listing[peer, kind]
            table_parts.append((peer * LEAF_DEV + jnp.maximum(incoming, 0)).astype(jnp.int32))
            present_parts.append(valid & (incoming >= 0))
        table_ids = jnp.concatenate(table_parts)
        present = jnp.concatenate(present_parts)
        source_points = positions[table_ids]
        source_charge = jnp.where(present[:, None], charges[table_ids], 0.0)
        slot_ids = lax.dynamic_slice_in_dim(near_slot, device * LEAF_DEV, LEAF_DEV, 0)
        targets = lax.dynamic_slice_in_dim(positions, device * LEAF_DEV, LEAF_DEV, 0)
        return near_field(targets, source_points, source_charge, slot_ids)
    near_pot, near_force = lax.map(per_device, jnp.arange(device_count, dtype=jnp.int32))
    near_pot = near_pot.reshape(LEAVES, LEAF)
    near_force = near_force.reshape(LEAVES, 3, LEAF)
    return (far_pot + near_pot, far_force + near_force)
```

```python
import math

import jax
import jax.numpy as jnp
from jax import lax
from jax.experimental import pallas as pl
from jax.experimental.pallas import tpu as pltpu
from jax.sharding import PartitionSpec as P

ORDER = 10
COEF = 121
CLASSES = 316
SOFTENING = 0.01
GX = 4
GY = 32
REACH = 3
WIDTH = 2 * REACH + 1
SLOTS = WIDTH * WIDTH
OWN = SLOTS // 2
TILES = 299
MESH = pl.DeviceIdType.MESH

far_offsets = [
    (a, b, c)
    for a in range(-3, 4)
    for b in range(-3, 4)
    for c in range(-3, 4)
    if max(abs(a), abs(b), abs(c)) > 1
]


def scale_of(degree, moment):
    return math.sqrt(math.factorial(degree + moment) * math.factorial(degree - moment))


def coef_index(degree, moment, imag=0):
    return degree * degree + (2 * moment - 1 + imag if moment else 0)


def harmonic_columns(x, y, z, order):
    radius_sq = x * x + y * y + z * z
    diag = (jnp.ones_like(x), None)
    for moment in range(order + 1):
        if moment == 1:
            diag = (-0.5 * x, -0.5 * y)
        elif moment > 1:
            factor = -0.5 / moment
            real, imag = diag
            diag = (factor * (x * real - y * imag), factor * (x * imag + y * real))
        yield moment, moment, diag[0], diag[1]
        two_back, one_back = None, diag
        for degree in range(moment + 1, order + 1):
            if degree == moment + 1:
                step = tuple(None if v is None else z * v for v in one_back)
            else:
                factor = 1.0 / ((degree - moment) * (degree + moment))
                zf = (factor * (2 * degree - 1)) * z
                rf = factor * radius_sq
                step = tuple(
                    None if v is None else zf * v - rf * w for v, w in zip(one_back, two_back)
                )
            yield degree, moment, step[0], step[1]
            two_back, one_back = one_back, step


def partners(i, j, t):
    pi = t // 6
    pj = (j // 2) * 2 - 2 + t % 6
    ok = (pj >= 0) & (pj < GY) & ((pi != i) | (pj != j))
    return pi, pj, ok


halo_moves = (
    [((1, 0), 9 + y, 1 + y) for y in range(2)]
    + [((-1, 0), 5 + y, 13 + y) for y in range(2)]
    + [((0, 1), 4 * x + 2, 4 * x) for x in (1, 2)]
    + [((0, -1), 4 * x + 1, 4 * x + 3) for x in (1, 2)]
    + [((1, 1), 10, 0), ((1, -1), 9, 3), ((-1, 1), 6, 12), ((-1, -1), 5, 15)]
)


def exchange_kernel(pos_ref, charge_ref, tab, mg, cnt, send_m, recv_m, send_h, recv_h):
    i = lax.axis_index("gx")
    j = lax.axis_index("gy")
    zero_tile = jnp.zeros((8, 128), jnp.float32)
    mg[...] = jnp.zeros(mg.shape, jnp.float32)
    for column in range(16):
        if column not in (5, 6, 9, 10):
            tab[column] = jnp.zeros(tab.shape[1:], jnp.float32)

    barrier = pltpu.get_barrier_semaphore()

    def signal_partner(t, count):
        pi, pj, ok = partners(i, j, t)

        @pl.when(ok)
        def _():
            pl.semaphore_signal(barrier, inc=1, device_id=(pi, pj), device_id_type=MESH)

        return count + ok.astype(jnp.int32)

    total = lax.fori_loop(0, 24, signal_partner, jnp.int32(0))
    for bx in range(2):
        for by in range(2):
            column = 4 * (1 + bx) + 1 + by
            for bz in range(2):
                rows = pl.ds(bx + 2 * by + 4 * bz, 8, stride=8)
                dest = pl.ds(bz, 8, stride=2)
                for comp in range(3):
                    tab[column, comp, dest, :] = pos_ref[comp, rows, :]
                tab[column, 3, dest, :] = charge_ref[rows, :]
    pl.semaphore_wait(barrier, total)

    def halo_copy(move, index):
        (da, db), source, dest = move
        return pltpu.make_async_remote_copy(
            src_ref=tab.at[source],
            dst_ref=tab.at[dest],
            send_sem=send_h.at[index],
            recv_sem=recv_h.at[index],
            device_id=(i + da, j + db),
            device_id_type=MESH,
        )

    def inside(a, b):
        return (i + a >= 0) & (i + a < GX) & (j + b >= 0) & (j + b < GY)

    for index, move in enumerate(halo_moves):

        @pl.when(inside(*move[0]))
        def _():
            halo_copy(move, index).start()

    cell = lax.broadcasted_iota(jnp.int32, (8, 128), 0).astype(jnp.float32)
    lane = lax.broadcasted_iota(jnp.int32, (8, 128), 1)
    stacked = [
        jnp.stack([pos_ref[comp, pl.ds(b, 8, stride=8), :] for b in range(8)]) for comp in range(3)
    ]
    charge = jnp.stack([charge_ref[pl.ds(b, 8, stride=8), :] for b in range(8)])
    x = stacked[0] - (2 * i + 1).astype(jnp.float32)
    y = stacked[1] - (2 * j + 1).astype(jnp.float32)
    z = stacked[2] - (2.0 * cell + 1.0)[None]
    moments = zero_tile
    for degree, moment, real, imag in harmonic_columns(x, y, z, ORDER):
        for part, value in enumerate((real, imag)):
            if value is None:
                continue
            summed = jnp.sum(jnp.sum(value * charge, axis=0), axis=1, keepdims=True)
            index = coef_index(degree, moment, part)
            moments = jnp.where(lane == index, scale_of(degree, moment) * summed, moments)
    mg[OWN] = moments.astype(jnp.bfloat16).astype(jnp.float32)

    def multipole_copy(pi, pj):
        there = (i - pi + REACH) * WIDTH + (j - pj + REACH)
        return pltpu.make_async_remote_copy(
            src_ref=mg.at[OWN],
            dst_ref=mg.at[there],
            send_sem=send_m.at[there],
            recv_sem=recv_m.at[there],
            device_id=(pi, pj),
            device_id_type=MESH,
        )

    def send_multipole(t, carry):
        pi, pj, ok = partners(i, j, t)

        @pl.when(ok)
        def _():
            multipole_copy(pi, pj).start()

        return carry

    lax.fori_loop(0, 24, send_multipole, 0)

    def wait_multipole(t, carry):
        pi, pj, ok = partners(i, j, t)

        @pl.when(ok)
        def _():
            multipole_copy(pi, pj).wait_send()
            here = (pi - i + REACH) * WIDTH + (pj - j + REACH)
            pltpu.make_async_remote_copy(
                src_ref=mg.at[OWN],
                dst_ref=mg.at[here],
                send_sem=send_m.at[here],
                recv_sem=recv_m.at[here],
                device_id=(pi, pj),
                device_id_type=MESH,
            ).wait_recv()

        return carry

    lax.fori_loop(0, 24, wait_multipole, 0)
    for index, move in enumerate(halo_moves):
        da, db = move[0]

        @pl.when(inside(da, db))
        def _():
            halo_copy(move, index).wait_send()

        @pl.when(inside(-da, -db))
        def _():
            halo_copy(move, index).wait_recv()

    counts = jnp.zeros((16, 128), jnp.int32)
    lanes = lax.broadcasted_iota(jnp.int32, (16, 128), 1)
    for column in range(16):
        used = jnp.where(tab[column, 3] != 0.0, lanes + 1, 0)
        counts = jnp.where(lanes == column, jnp.max(used, axis=1, keepdims=True), counts)
    cnt[...] = counts


def exchange(pos, charges):
    vmem = pl.BlockSpec(memory_space=pltpu.VMEM)
    return pl.pallas_call(
        exchange_kernel,
        out_shape=(
            jax.ShapeDtypeStruct((16, 4, 16, 128), jnp.float32),
            jax.ShapeDtypeStruct((SLOTS, 8, 128), jnp.float32),
            jax.ShapeDtypeStruct((16, 128), jnp.int32),
        ),
        in_specs=[vmem, vmem],
        out_specs=(vmem, vmem, vmem),
        scratch_shapes=[
            pltpu.SemaphoreType.DMA((SLOTS,)),
            pltpu.SemaphoreType.DMA((SLOTS,)),
            pltpu.SemaphoreType.DMA((len(halo_moves),)),
            pltpu.SemaphoreType.DMA((len(halo_moves),)),
        ],
        compiler_params=pltpu.CompilerParams(
            collective_id=0, has_side_effects=True, vmem_limit_bytes=40 << 20
        ),
        name="exchange",
    )(pos, charges)


source_lists = [
    ((5, 6, 9, 10), (5, 6, 9, 10)),
    ((1, 2), (5, 6)),
    ((13, 14), (9, 10)),
    ((4, 8), (5, 9)),
    ((7, 11), (6, 10)),
    ((0,), (5,)),
    ((3,), (6,)),
    ((12,), (9,)),
    ((15,), (10,)),
]
own_columns = (5, 6, 9, 10)
unrolls = {4: 4, 2: 8, 1: 8}
list_rows = [(len(sources) * 16 + 1) * 128 for sources, _ in source_lists]
list_base = [sum(list_rows[:n]) for n in range(len(list_rows))]
TABLE_ROWS = sum(list_rows)


def build_sources(tab, cnt, columns, table, starts):
    for column in range(16):
        flat = tab[column].reshape(64, 128)
        columns[column] = jnp.transpose(jnp.concatenate([flat, flat], axis=0))

    def step(z, offsets):
        offsets = list(offsets)
        for n, (sources, _) in enumerate(source_lists):
            starts[n, z] = offsets[n]
            for column in sources:
                rows = pl.ds(pl.multiple_of(list_base[n] + offsets[n] * 8, 8), 128)
                table[rows, :] = pltpu.roll(columns[column], (128 - z) % 128, 1)
                offsets[n] = offsets[n] + (cnt[z, column] + 7) // 8
        return tuple(offsets)

    ends = lax.fori_loop(0, 16, step, (jnp.int32(0),) * len(source_lists))
    for n, end in enumerate(ends):
        starts[n, 16] = end
        rows = pl.ds(pl.multiple_of(list_base[n] + end * 8, 8), 128)
        table[rows, :] = jnp.zeros((128, 128), jnp.float32)


def near_field(tab, table, starts, near):
    def step(z, carry):
        for n, (_, targets) in enumerate(source_lists):
            unroll = unrolls[len(targets)]
            first = starts[n, jnp.maximum(z - 1, 0)]
            last = starts[n, jnp.minimum(z + 2, 16)]
            at = [
                [jnp.broadcast_to(tab[t, comp, pl.ds(z, 1), :], (8, 128)) for comp in range(3)]
                for t in targets
            ]
            if n == 0:
                init = tuple(jnp.zeros((8, 128), jnp.float32) for _ in range(4 * len(targets)))
            else:
                init = tuple(near[comp, t, z] for t in targets for comp in range(4))

            def body(it, sums):
                sums = list(sums)
                granule = first + it * unroll
                rows = table[
                    pl.ds(pl.multiple_of(list_base[n] + granule * 8, 8), 8 * unroll), :
                ]
                for u in range(unroll):
                    piece = rows[8 * u : 8 * u + 8]
                    xs, ys, zs, cs = (
                        jnp.broadcast_to(piece[:, k : k + 1], (8, 128)) for k in (0, 16, 32, 48)
                    )
                    cs = jnp.where(granule + u < last, cs, 0.0)
                    for k in range(len(targets)):
                        dx = at[k][0] - xs
                        dy = at[k][1] - ys
                        dz = at[k][2] - zs
                        inverse = lax.rsqrt(dx * dx + dy * dy + (dz * dz + SOFTENING))
                        weight = cs * inverse
                        cubed = weight * (inverse * inverse)
                        sums[4 * k] += weight
                        sums[4 * k + 1] += cubed * dx
                        sums[4 * k + 2] += cubed * dy
                        sums[4 * k + 3] += cubed * dz
                return tuple(sums)

            sums = lax.fori_loop(0, (last - first + unroll - 1) // unroll, body, init)
            for k, t in enumerate(targets):
                for comp in range(4):
                    near[comp, t, z] = sums[4 * k + comp]
        return carry

    lax.fori_loop(0, 16, step, 0)


def stack_multipoles(mg, padded, stacked):
    cell = lax.broadcasted_iota(jnp.int32, (8, 128), 0)
    lane = lax.broadcasted_iota(jnp.int32, (8, 128), 1)
    padded[...] = jnp.zeros(padded.shape, jnp.float32)
    for s in range(SLOTS):
        padded[s, 8:16, :] = mg[s]
    even = cell % 2 == 0
    current = jnp.zeros((8, 128), jnp.float32)
    for k, (a, b, c) in enumerate(far_offsets):
        value = padded[(a + REACH) * WIDTH + b + REACH, 8 + c : 16 + c, :]
        if c == 3:
            value = jnp.where(even, value, 0.0)
        elif c == -3:
            value = jnp.where(even, 0.0, value)
        tile, shift = divmod(k * COEF, 128)
        rolled = pltpu.roll(value, shift, 1) if shift else value
        current = jnp.where(lane >= shift, rolled, current)
        if shift + COEF >= 128:
            stacked[:, tile * 128 : tile * 128 + 128] = current
            current = rolled
    last = CLASSES * COEF
    tile, shift = divmod(last, 128)
    if shift:
        stacked[:, tile * 128 : tile * 128 + 128] = jnp.where(lane < shift, current, 0.0)


CHUNK = 4096


def local_expansion(stacked, operator):
    total = jnp.zeros((8, COEF), jnp.float32)
    width = CLASSES * COEF
    for start in range(0, width, CHUNK):
        stop = min(start + CHUNK, width)
        total += lax.dot_general(
            stacked[:, start:stop].astype(jnp.bfloat16),
            operator[:, start:stop],
            (((1,), (1,)), ((), ())),
            preferred_element_type=jnp.float32,
        )
    return total


def far_tables(local, coefs):
    def factor(degree, moment):
        if degree > ORDER or moment > degree:
            return None
        scale = scale_of(degree, moment)
        pick = lambda index: jnp.broadcast_to(local[:, index : index + 1], (8, 128)) * scale
        real = pick(coef_index(degree, moment))
        imag = -pick(coef_index(degree, moment, 1)) if moment else None
        return real, imag

    zero = jnp.zeros((8, 128), jnp.float32)
    index = 0
    for moment in range(ORDER + 1):
        for degree in range(moment, ORDER + 1):
            own = factor(degree, moment)
            coefs[0, index, 0] = own[0]
            if moment:
                coefs[0, index, 1] = own[1]
            if degree < ORDER:
                below = factor(degree + 1, moment - 1) if moment else None
                above = factor(degree + 1, moment + 1)
                level = factor(degree + 1, moment)
                weight = 1.0 if moment == 1 else 0.5
                low = (zero, zero)
                if below:
                    low = (weight * below[0], zero if below[1] is None else weight * below[1])
                high = (0.5 * above[0], 0.5 * above[1])
                coefs[1, index, 0] = low[0] - high[0]
                coefs[2, index, 0] = low[1] + high[1]
                coefs[3, index, 0] = level[0]
                if moment:
                    coefs[1, index, 1] = low[1] - high[1]
                    coefs[2, index, 1] = -(low[0] + high[0])
                    coefs[3, index, 1] = level[1]
            index += 1


def finish(tab, near, coefs, pot_ref, field_ref):
    i = lax.axis_index("gx")
    j = lax.axis_index("gy")
    cell = lax.broadcasted_iota(jnp.int32, (8, 128), 0).astype(jnp.float32)
    self_term = lax.rsqrt(jnp.full((8, 128), SOFTENING, jnp.float32))
    for bz in range(2):
        rows = pl.ds(bz, 8, stride=2)
        pick = lambda comp: jnp.stack([tab[t, comp, rows, :] for t in own_columns])
        x = pick(0) - (2 * i + 1).astype(jnp.float32)
        y = pick(1) - (2 * j + 1).astype(jnp.float32)
        z = pick(2) - (2.0 * cell + 1.0)[None]
        sums = [jnp.zeros((4, 8, 128), jnp.float32) for _ in range(4)]
        index = 0
        for degree, moment, real, imag in harmonic_columns(x, y, z, ORDER):
            for out in range(4 if degree < ORDER else 1):
                sums[out] += coefs[out, index, 0][None] * real
                if moment:
                    sums[out] -= coefs[out, index, 1][None] * imag
            index += 1
        for k, t in enumerate(own_columns):
            leaf = (t // 4 - 1) + 2 * (t % 4 - 1) + 4 * bz
            dest = pl.ds(leaf, 8, stride=8)
            pair = [near[comp, t, rows] for comp in range(4)]
            close = [jnp.sum(v, axis=1) for v in pair]
            charge = tab[t, 3, rows, :]
            pot_ref[dest, :] = sums[0][k] + (close[0] - charge * self_term)
            for comp in range(3):
                field_ref[comp, dest, :] = close[comp + 1] - sums[comp + 1][k]


def evaluate_kernel(
    cnt, tab, mg, translations, pot_ref, field_ref,
    columns, table, starts, near, padded, stacked, operator, coefs, copy_sem,
):
    fetch = pltpu.make_async_copy(translations, operator, copy_sem)
    fetch.start()
    build_sources(tab, cnt, columns, table, starts)
    near_field(tab, table, starts, near)
    stack_multipoles(mg, padded, stacked)
    fetch.wait()
    local = local_expansion(stacked, operator)
    far_tables(local, coefs)
    finish(tab, near, coefs, pot_ref, field_ref)


def evaluate(cnt, tab, mg, translations):
    vmem = pl.BlockSpec(memory_space=pltpu.VMEM)
    f32 = jnp.float32
    return pl.pallas_call(
        evaluate_kernel,
        out_shape=(
            jax.ShapeDtypeStruct((64, 128), f32),
            jax.ShapeDtypeStruct((3, 64, 128), f32),
        ),
        in_specs=[
            pl.BlockSpec(memory_space=pltpu.SMEM),
            vmem,
            vmem,
            pl.BlockSpec(memory_space=pl.ANY),
        ],
        out_specs=(vmem, vmem),
        scratch_shapes=[
            pltpu.VMEM((16, 128, 128), f32),
            pltpu.VMEM((TABLE_ROWS, 128), f32),
            pltpu.SMEM((len(source_lists), 17), jnp.int32),
            pltpu.VMEM((4, 16, 16, 8, 128), f32),
            pltpu.VMEM((SLOTS, 24, 128), f32),
            pltpu.VMEM((8, TILES * 128), f32),
            pltpu.VMEM((COEF, CLASSES * COEF), jnp.bfloat16),
            pltpu.VMEM((4, 66, 2, 8, 128), f32),
            pltpu.SemaphoreType.DMA,
        ],
        compiler_params=pltpu.CompilerParams(vmem_limit_bytes=56 << 20),
        name="evaluate",
    )(cnt, tab, mg, translations)


def per_device(
    positions, charges, send_x, send_y, send_corner, near_slot, far_sources, translations
):
    tab, mg, cnt = exchange(jnp.transpose(positions, (1, 0, 2)), charges)
    potential, field = evaluate(cnt, tab, mg, translations)
    return potential, jnp.transpose(field, (1, 0, 2))


def solution(mesh):
    return jax.shard_map(
        per_device,
        mesh=mesh,
        in_specs=(
            P(("gx", "gy"), None, None),
            P(("gx", "gy"), None),
            P(("gx", "gy"), None, None),
            P(("gx", "gy"), None, None),
            P(("gx", "gy"), None, None),
            P(("gx", "gy"), None),
            P(("gx", "gy"), None),
            P(),
        ),
        out_specs=(P(("gx", "gy"), None), P(("gx", "gy"), None, None)),
        check_vma=False,
    )
```

```python
import math

import jax
import jax.numpy as jnp
from jax import lax
from jax.experimental import pallas as pl
from jax.experimental.pallas import tpu as pltpu
from jax.sharding import PartitionSpec as P

ORDER = 10
COEF = 121
CLASSES = 316
SOFTENING = 0.01
GX = 4
GY = 32
REACH = 3
WIDTH = 2 * REACH + 1
SLOTS = WIDTH * WIDTH
OWN = SLOTS // 2
TILES = 299
MESH = pl.DeviceIdType.MESH

far_offsets = [
    (a, b, c)
    for a in range(-3, 4)
    for b in range(-3, 4)
    for c in range(-3, 4)
    if max(abs(a), abs(b), abs(c)) > 1
]


def scale_of(degree, moment):
    return math.sqrt(math.factorial(degree + moment) * math.factorial(degree - moment))


def coef_index(degree, moment, imag=0):
    return degree * degree + (2 * moment - 1 + imag if moment else 0)


def harmonic_columns(x, y, z, order):
    radius_sq = x * x + y * y + z * z
    diag = (jnp.ones_like(x), None)
    for moment in range(order + 1):
        if moment == 1:
            diag = (-0.5 * x, -0.5 * y)
        elif moment > 1:
            factor = -0.5 / moment
            real, imag = diag
            diag = (factor * (x * real - y * imag), factor * (x * imag + y * real))
        yield moment, moment, diag[0], diag[1]
        two_back, one_back = None, diag
        for degree in range(moment + 1, order + 1):
            if degree == moment + 1:
                step = tuple(None if v is None else z * v for v in one_back)
            else:
                factor = 1.0 / ((degree - moment) * (degree + moment))
                zf = (factor * (2 * degree - 1)) * z
                rf = factor * radius_sq
                step = tuple(
                    None if v is None else zf * v - rf * w for v, w in zip(one_back, two_back)
                )
            yield degree, moment, step[0], step[1]
            two_back, one_back = one_back, step


def partners(i, j, t):
    pi = t // 6
    pj = (j // 2) * 2 - 2 + t % 6
    ok = (pj >= 0) & (pj < GY) & ((pi != i) | (pj != j))
    return pi, pj, ok


halo_moves = (
    [((1, 0), 9 + y, 1 + y) for y in range(2)]
    + [((-1, 0), 5 + y, 13 + y) for y in range(2)]
    + [((0, 1), 4 * x + 2, 4 * x) for x in (1, 2)]
    + [((0, -1), 4 * x + 1, 4 * x + 3) for x in (1, 2)]
    + [((1, 1), 10, 0), ((1, -1), 9, 3), ((-1, 1), 6, 12), ((-1, -1), 5, 15)]
)


def exchange_kernel(pos_ref, charge_ref, tab, mg, cnt, send_m, recv_m, send_h, recv_h):
    i = lax.axis_index("gx")
    j = lax.axis_index("gy")
    zero_tile = jnp.zeros((8, 128), jnp.float32)
    mg[...] = jnp.zeros(mg.shape, jnp.float32)
    for column in range(16):
        if column not in (5, 6, 9, 10):
            tab[column] = jnp.zeros(tab.shape[1:], jnp.float32)

    barrier = pltpu.get_barrier_semaphore()

    def signal_partner(t, count):
        pi, pj, ok = partners(i, j, t)

        @pl.when(ok)
        def _():
            pl.semaphore_signal(barrier, inc=1, device_id=(pi, pj), device_id_type=MESH)

        return count + ok.astype(jnp.int32)

    total = lax.fori_loop(0, 24, signal_partner, jnp.int32(0))
    for bx in range(2):
        for by in range(2):
            column = 4 * (1 + bx) + 1 + by
            for bz in range(2):
                rows = pl.ds(bx + 2 * by + 4 * bz, 8, stride=8)
                dest = pl.ds(bz, 8, stride=2)
                for comp in range(3):
                    tab[column, comp, dest, :] = pos_ref[comp, rows, :]
                tab[column, 3, dest, :] = charge_ref[rows, :]
    pl.semaphore_wait(barrier, total)

    def halo_copy(move, index):
        (da, db), source, dest = move
        return pltpu.make_async_remote_copy(
            src_ref=tab.at[source],
            dst_ref=tab.at[dest],
            send_sem=send_h.at[index],
            recv_sem=recv_h.at[index],
            device_id=(i + da, j + db),
            device_id_type=MESH,
        )

    def inside(a, b):
        return (i + a >= 0) & (i + a < GX) & (j + b >= 0) & (j + b < GY)

    for index, move in enumerate(halo_moves):

        @pl.when(inside(*move[0]))
        def _():
            halo_copy(move, index).start()

    cell = lax.broadcasted_iota(jnp.int32, (8, 128), 0).astype(jnp.float32)
    lane = lax.broadcasted_iota(jnp.int32, (8, 128), 1)
    stacked = [
        jnp.stack([pos_ref[comp, pl.ds(b, 8, stride=8), :] for b in range(8)]) for comp in range(3)
    ]
    charge = jnp.stack([charge_ref[pl.ds(b, 8, stride=8), :] for b in range(8)])
    x = stacked[0] - (2 * i + 1).astype(jnp.float32)
    y = stacked[1] - (2 * j + 1).astype(jnp.float32)
    z = stacked[2] - (2.0 * cell + 1.0)[None]
    moments = zero_tile
    for degree, moment, real, imag in harmonic_columns(x, y, z, ORDER):
        for part, value in enumerate((real, imag)):
            if value is None:
                continue
            summed = jnp.sum(jnp.sum(value * charge, axis=0), axis=1, keepdims=True)
            index = coef_index(degree, moment, part)
            moments = jnp.where(lane == index, scale_of(degree, moment) * summed, moments)
    mg[OWN] = moments.astype(jnp.bfloat16).astype(jnp.float32)

    def multipole_copy(pi, pj):
        there = (i - pi + REACH) * WIDTH + (j - pj + REACH)
        return pltpu.make_async_remote_copy(
            src_ref=mg.at[OWN],
            dst_ref=mg.at[there],
            send_sem=send_m.at[there],
            recv_sem=recv_m.at[there],
            device_id=(pi, pj),
            device_id_type=MESH,
        )

    def send_multipole(t, carry):
        pi, pj, ok = partners(i, j, t)

        @pl.when(ok)
        def _():
            multipole_copy(pi, pj).start()

        return carry

    lax.fori_loop(0, 24, send_multipole, 0)

    def wait_multipole(t, carry):
        pi, pj, ok = partners(i, j, t)

        @pl.when(ok)
        def _():
            multipole_copy(pi, pj).wait_send()
            here = (pi - i + REACH) * WIDTH + (pj - j + REACH)
            pltpu.make_async_remote_copy(
                src_ref=mg.at[OWN],
                dst_ref=mg.at[here],
                send_sem=send_m.at[here],
                recv_sem=recv_m.at[here],
                device_id=(pi, pj),
                device_id_type=MESH,
            ).wait_recv()

        return carry

    lax.fori_loop(0, 24, wait_multipole, 0)
    for index, move in enumerate(halo_moves):
        da, db = move[0]

        @pl.when(inside(da, db))
        def _():
            halo_copy(move, index).wait_send()

        @pl.when(inside(-da, -db))
        def _():
            halo_copy(move, index).wait_recv()

    counts = jnp.zeros((16, 128), jnp.int32)
    lanes = lax.broadcasted_iota(jnp.int32, (16, 128), 1)
    for column in range(16):
        used = jnp.where(tab[column, 3] != 0.0, lanes + 1, 0)
        counts = jnp.where(lanes == column, jnp.max(used, axis=1, keepdims=True), counts)
    cnt[...] = counts


def exchange(pos, charges):
    vmem = pl.BlockSpec(memory_space=pltpu.VMEM)
    return pl.pallas_call(
        exchange_kernel,
        out_shape=(
            jax.ShapeDtypeStruct((16, 4, 16, 128), jnp.float32),
            jax.ShapeDtypeStruct((SLOTS, 8, 128), jnp.float32),
            jax.ShapeDtypeStruct((16, 128), jnp.int32),
        ),
        in_specs=[vmem, vmem],
        out_specs=(vmem, vmem, vmem),
        scratch_shapes=[
            pltpu.SemaphoreType.DMA((SLOTS,)),
            pltpu.SemaphoreType.DMA((SLOTS,)),
            pltpu.SemaphoreType.DMA((len(halo_moves),)),
            pltpu.SemaphoreType.DMA((len(halo_moves),)),
        ],
        compiler_params=pltpu.CompilerParams(
            collective_id=0, has_side_effects=True, vmem_limit_bytes=40 << 20
        ),
        name="exchange",
    )(pos, charges)


source_lists = [
    ((5, 6, 9, 10), (5, 6, 9, 10)),
    ((1, 2), (5, 6)),
    ((13, 14), (9, 10)),
    ((4, 8), (5, 9)),
    ((7, 11), (6, 10)),
    ((0,), (5,)),
    ((3,), (6,)),
    ((12,), (9,)),
    ((15,), (10,)),
]
own_columns = (5, 6, 9, 10)
unrolls = {4: 8, 2: 8, 1: 8}
ring_slots = [4 * 16 * len(sources) for sources, _ in source_lists]
ring_base = [sum(ring_slots[:n]) for n in range(len(ring_slots))]
RING = sum(ring_slots)


def build_sources(cnt, columns, starts, ring, z):
    row = lax.broadcasted_iota(jnp.int32, (256, 512), 0)
    comp_of = lax.broadcasted_iota(jnp.int32, (256, 512), 1) // 128
    pick = ((row % 64 == comp_of * 16 + z) & (row < 192)).astype(jnp.float32).astype(jnp.bfloat16)
    for n, (sources, _) in enumerate(source_lists):
        base = sum(len(s) for s, _ in source_lists[:n]) * 128
        spread = jnp.dot(
            columns[base : base + 128 * len(sources), :], pick, preferred_element_type=jnp.float32
        )
        offset = starts[n, z]
        for k, column in enumerate(sources):
            for g in range(16):
                slot = ring_base[n] + ((offset + g) & (ring_slots[n] - 1))
                rows = slice(128 * k + 8 * g, 128 * k + 8 * g + 8)
                for comp in range(4):
                    ring[slot, comp] = spread[rows, 128 * comp : 128 * comp + 128]
            offset = offset + (cnt[z, column] + 7) // 8
        starts[n, z + 1] = offset


def near_slab(tab, starts, ring, near, z):
    for n, (_, targets) in enumerate(source_lists):
        unroll = unrolls[len(targets)]
        first = starts[n, jnp.maximum(z - 1, 0)]
        last = starts[n, jnp.minimum(z + 2, 16)]
        at = [
            [jnp.broadcast_to(tab[t, comp, pl.ds(z, 1), :], (8, 128)) for comp in range(3)]
            for t in targets
        ]
        if n == 0:
            init = tuple(jnp.zeros((8, 128), jnp.float32) for _ in range(4 * len(targets)))
        else:
            init = tuple(near[comp, t, z] for t in targets for comp in range(4))

        def body(it, sums):
            sums = list(sums)
            for u in range(unroll):
                granule = first + it * unroll + u
                slot = ring_base[n] + (jnp.minimum(granule, last - 1) & (ring_slots[n] - 1))
                xs, ys, zs, cs = (ring[slot, comp] for comp in range(4))
                cs = jnp.where(granule < last, cs, 0.0)
                for k in range(len(targets)):
                    dx = at[k][0] - xs
                    dy = at[k][1] - ys
                    dz = at[k][2] - zs
                    inverse = lax.rsqrt(dx * dx + dy * dy + (dz * dz + SOFTENING))
                    weight = cs * inverse
                    cubed = weight * (inverse * inverse)
                    sums[4 * k] += weight
                    sums[4 * k + 1] += cubed * dx
                    sums[4 * k + 2] += cubed * dy
                    sums[4 * k + 3] += cubed * dz
            return tuple(sums)

        sums = lax.fori_loop(0, (last - first + unroll - 1) // unroll, body, init)
        for k, t in enumerate(targets):
            for comp in range(4):
                near[comp, t, z] = sums[4 * k + comp]


def near_field(tab, cnt, columns, starts, ring, near):
    low_lanes = lax.broadcasted_iota(jnp.int32, (128, 128), 1) < 64
    order = [column for sources, _ in source_lists for column in sources]
    for place, column in enumerate(order):
        flat = tab[column].reshape(64, 128)
        value = jnp.transpose(jnp.concatenate([flat, flat], axis=0))
        high = value.astype(jnp.bfloat16).astype(jnp.float32)
        rest = value - high
        middle = rest.astype(jnp.bfloat16).astype(jnp.float32)
        rows = slice(128 * place, 128 * place + 128)
        columns[rows, :128] = jnp.where(low_lanes, high, middle).astype(jnp.bfloat16)
        columns[rows, 128:] = jnp.where(low_lanes, rest - middle, 0.0).astype(jnp.bfloat16)
    for n in range(len(source_lists)):
        starts[n, 0] = 0

    def step(z, carry):
        @pl.when(z < 16)
        def _():
            build_sources(cnt, columns, starts, ring, z)

        @pl.when(z > 0)
        def _():
            near_slab(tab, starts, ring, near, z - 1)

        return carry

    lax.fori_loop(0, 17, step, 0)


def stack_multipoles(mg, padded, stacked):
    cell = lax.broadcasted_iota(jnp.int32, (8, 128), 0)
    lane = lax.broadcasted_iota(jnp.int32, (8, 128), 1)
    padded[...] = jnp.zeros(padded.shape, jnp.float32)
    for s in range(SLOTS):
        padded[s, 8:16, :] = mg[s]
    even = cell % 2 == 0
    current = jnp.zeros((8, 128), jnp.float32)
    for k, (a, b, c) in enumerate(far_offsets):
        value = padded[(a + REACH) * WIDTH + b + REACH, 8 + c : 16 + c, :]
        if c == 3:
            value = jnp.where(even, value, 0.0)
        elif c == -3:
            value = jnp.where(even, 0.0, value)
        tile, shift = divmod(k * COEF, 128)
        rolled = pltpu.roll(value, shift, 1) if shift else value
        current = jnp.where(lane >= shift, rolled, current)
        if shift + COEF >= 128:
            stacked[:, tile * 128 : tile * 128 + 128] = current
            current = rolled
    last = CLASSES * COEF
    tile, shift = divmod(last, 128)
    if shift:
        stacked[:, tile * 128 : tile * 128 + 128] = jnp.where(lane < shift, current, 0.0)


CHUNK = 4096


def local_expansion(stacked, operator):
    total = jnp.zeros((8, COEF), jnp.float32)
    width = CLASSES * COEF
    for start in range(0, width, CHUNK):
        stop = min(start + CHUNK, width)
        total += lax.dot_general(
            stacked[:, start:stop].astype(jnp.bfloat16),
            operator[start:stop, :],
            (((1,), (0,)), ((), ())),
            preferred_element_type=jnp.float32,
        )
    return total


def far_tables(local, coefs):
    def factor(degree, moment):
        if degree > ORDER or moment > degree:
            return None
        scale = scale_of(degree, moment)
        pick = lambda index: jnp.broadcast_to(local[:, index : index + 1], (8, 128)) * scale
        real = pick(coef_index(degree, moment))
        imag = -pick(coef_index(degree, moment, 1)) if moment else None
        return real, imag

    zero = jnp.zeros((8, 128), jnp.float32)
    index = 0
    for moment in range(ORDER + 1):
        for degree in range(moment, ORDER + 1):
            own = factor(degree, moment)
            coefs[0, index, 0] = own[0]
            if moment:
                coefs[0, index, 1] = own[1]
            if degree < ORDER:
                below = factor(degree + 1, moment - 1) if moment else None
                above = factor(degree + 1, moment + 1)
                level = factor(degree + 1, moment)
                weight = 1.0 if moment == 1 else 0.5
                low = (zero, zero)
                if below:
                    low = (weight * below[0], zero if below[1] is None else weight * below[1])
                high = (0.5 * above[0], 0.5 * above[1])
                coefs[1, index, 0] = low[0] - high[0]
                coefs[2, index, 0] = low[1] + high[1]
                coefs[3, index, 0] = level[0]
                if moment:
                    coefs[1, index, 1] = low[1] - high[1]
                    coefs[2, index, 1] = -(low[0] + high[0])
                    coefs[3, index, 1] = level[1]
            index += 1


def finish(tab, near, coefs, pot_ref, field_ref):
    i = lax.axis_index("gx")
    j = lax.axis_index("gy")
    cell = lax.broadcasted_iota(jnp.int32, (8, 128), 0).astype(jnp.float32)
    self_term = lax.rsqrt(jnp.full((8, 128), SOFTENING, jnp.float32))
    for bz in range(2):
        rows = pl.ds(bz, 8, stride=2)
        pick = lambda comp: jnp.stack([tab[t, comp, rows, :] for t in own_columns])
        x = pick(0) - (2 * i + 1).astype(jnp.float32)
        y = pick(1) - (2 * j + 1).astype(jnp.float32)
        z = pick(2) - (2.0 * cell + 1.0)[None]
        sums = [jnp.zeros((4, 8, 128), jnp.float32) for _ in range(4)]
        index = 0
        for degree, moment, real, imag in harmonic_columns(x, y, z, ORDER):
            for out in range(4 if degree < ORDER else 1):
                sums[out] += coefs[out, index, 0][None] * real
                if moment:
                    sums[out] -= coefs[out, index, 1][None] * imag
            index += 1
        for k, t in enumerate(own_columns):
            leaf = (t // 4 - 1) + 2 * (t % 4 - 1) + 4 * bz
            dest = pl.ds(leaf, 8, stride=8)
            pair = [near[comp, t, rows] for comp in range(4)]
            close = [jnp.sum(v, axis=1) for v in pair]
            charge = tab[t, 3, rows, :]
            pot_ref[dest, :] = sums[0][k] + (close[0] - charge * self_term)
            for comp in range(3):
                field_ref[comp, dest, :] = close[comp + 1] - sums[comp + 1][k]


def evaluate_kernel(
    cnt, tab, mg, translations, pot_ref, field_ref,
    columns, starts, ring, near, padded, stacked, operator, coefs, copy_sem,
):
    fetch = pltpu.make_async_copy(translations, operator, copy_sem)
    fetch.start()
    near_field(tab, cnt, columns, starts, ring, near)
    stack_multipoles(mg, padded, stacked)
    fetch.wait()
    local = local_expansion(stacked, operator)
    far_tables(local, coefs)
    finish(tab, near, coefs, pot_ref, field_ref)


def evaluate(cnt, tab, mg, translations):
    vmem = pl.BlockSpec(memory_space=pltpu.VMEM)
    f32 = jnp.float32
    return pl.pallas_call(
        evaluate_kernel,
        out_shape=(
            jax.ShapeDtypeStruct((64, 128), f32),
            jax.ShapeDtypeStruct((3, 64, 128), f32),
        ),
        in_specs=[
            pl.BlockSpec(memory_space=pltpu.SMEM),
            vmem,
            vmem,
            pl.BlockSpec(memory_space=pl.ANY),
        ],
        out_specs=(vmem, vmem),
        scratch_shapes=[
            pltpu.VMEM((2048, 256), jnp.bfloat16),
            pltpu.SMEM((len(source_lists), 17), jnp.int32),
            pltpu.VMEM((RING, 4, 8, 128), f32),
            pltpu.VMEM((4, 16, 16, 8, 128), f32),
            pltpu.VMEM((SLOTS, 24, 128), f32),
            pltpu.VMEM((8, TILES * 128), f32),
            pltpu.VMEM((CLASSES * COEF, COEF), jnp.bfloat16),
            pltpu.VMEM((4, 66, 2, 8, 128), f32),
            pltpu.SemaphoreType.DMA,
        ],
        compiler_params=pltpu.CompilerParams(vmem_limit_bytes=58 << 20),
        name="evaluate",
    )(cnt, tab, mg, translations)


def per_device(
    positions, charges, send_x, send_y, send_corner, near_slot, far_sources, translations
):
    tab, mg, cnt = exchange(jnp.transpose(positions, (1, 0, 2)), charges)
    potential, field = evaluate(cnt, tab, mg, jnp.transpose(translations))
    return potential, jnp.transpose(field, (1, 0, 2))


def solution(mesh):
    return jax.shard_map(
        per_device,
        mesh=mesh,
        in_specs=(
            P(("gx", "gy"), None, None),
            P(("gx", "gy"), None),
            P(("gx", "gy"), None, None),
            P(("gx", "gy"), None, None),
            P(("gx", "gy"), None, None),
            P(("gx", "gy"), None),
            P(("gx", "gy"), None),
            P(),
        ),
        out_specs=(P(("gx", "gy"), None), P(("gx", "gy"), None, None)),
        check_vma=False,
    )
```

```python
import math

import jax
import jax.numpy as jnp
from jax import lax
from jax.experimental import pallas as pl
from jax.experimental.pallas import tpu as pltpu
from jax.sharding import PartitionSpec as P

ORDER = 10
COEF = 121
CLASSES = 316
SOFTENING = 0.01
GX = 4
GY = 32
REACH = 3
WIDTH = 2 * REACH + 1
SLOTS = WIDTH * WIDTH
OWN = SLOTS // 2
TILES = 299
MESH = pl.DeviceIdType.MESH

far_offsets = [
    (a, b, c)
    for a in range(-3, 4)
    for b in range(-3, 4)
    for c in range(-3, 4)
    if max(abs(a), abs(b), abs(c)) > 1
]


def scale_of(degree, moment):
    return math.sqrt(math.factorial(degree + moment) * math.factorial(degree - moment))


def coef_index(degree, moment, imag=0):
    return degree * degree + (2 * moment - 1 + imag if moment else 0)


def harmonic_columns(x, y, z, order):
    radius_sq = x * x + y * y + z * z
    diag = (jnp.ones_like(x), None)
    for moment in range(order + 1):
        if moment == 1:
            diag = (-0.5 * x, -0.5 * y)
        elif moment > 1:
            factor = -0.5 / moment
            real, imag = diag
            diag = (factor * (x * real - y * imag), factor * (x * imag + y * real))
        yield moment, moment, diag[0], diag[1]
        two_back, one_back = None, diag
        for degree in range(moment + 1, order + 1):
            if degree == moment + 1:
                step = tuple(None if v is None else z * v for v in one_back)
            else:
                factor = 1.0 / ((degree - moment) * (degree + moment))
                zf = (factor * (2 * degree - 1)) * z
                rf = factor * radius_sq
                step = tuple(
                    None if v is None else zf * v - rf * w for v, w in zip(one_back, two_back)
                )
            yield degree, moment, step[0], step[1]
            two_back, one_back = one_back, step


def partners(i, j, t):
    pi = t // 6
    pj = (j // 2) * 2 - 2 + t % 6
    ok = (pj >= 0) & (pj < GY) & ((pi != i) | (pj != j))
    return pi, pj, ok


halo_moves = (
    [((1, 0), 9 + y, 1 + y) for y in range(2)]
    + [((-1, 0), 5 + y, 13 + y) for y in range(2)]
    + [((0, 1), 4 * x + 2, 4 * x) for x in (1, 2)]
    + [((0, -1), 4 * x + 1, 4 * x + 3) for x in (1, 2)]
    + [((1, 1), 10, 0), ((1, -1), 9, 3), ((-1, 1), 6, 12), ((-1, -1), 5, 15)]
)


def exchange_kernel(
    pos_any, charge_any, tab, mg, cnt,
    pos_ref, charge_ref, fetch_sem, send_m, recv_m, send_h, recv_h,
):
    i = lax.axis_index("gx")
    j = lax.axis_index("gy")
    zero_tile = jnp.zeros((8, 128), jnp.float32)
    fetches = [
        pltpu.make_async_copy(pos_any, pos_ref, fetch_sem.at[0]),
        pltpu.make_async_copy(charge_any, charge_ref, fetch_sem.at[1]),
    ]
    for fetch in fetches:
        fetch.start()
    mg[...] = jnp.zeros(mg.shape, jnp.float32)
    for column in range(16):
        if column not in (5, 6, 9, 10):
            tab[column] = jnp.zeros(tab.shape[1:], jnp.float32)

    barrier = pltpu.get_barrier_semaphore()

    def signal_partner(t, count):
        pi, pj, ok = partners(i, j, t)

        @pl.when(ok)
        def _():
            pl.semaphore_signal(barrier, inc=1, device_id=(pi, pj), device_id_type=MESH)

        return count + ok.astype(jnp.int32)

    total = lax.fori_loop(0, 24, signal_partner, jnp.int32(0))
    for fetch in fetches:
        fetch.wait()
    for bx in range(2):
        for by in range(2):
            column = 4 * (1 + bx) + 1 + by
            for bz in range(2):
                rows = pl.ds(bx + 2 * by + 4 * bz, 8, stride=8)
                dest = pl.ds(bz, 8, stride=2)
                for comp in range(3):
                    tab[column, comp, dest, :] = pos_ref[comp, rows, :]
                tab[column, 3, dest, :] = charge_ref[rows, :]
    pl.semaphore_wait(barrier, total)

    def halo_copy(move, index):
        (da, db), source, dest = move
        return pltpu.make_async_remote_copy(
            src_ref=tab.at[source],
            dst_ref=tab.at[dest],
            send_sem=send_h.at[index],
            recv_sem=recv_h.at[index],
            device_id=(i + da, j + db),
            device_id_type=MESH,
        )

    def inside(a, b):
        return (i + a >= 0) & (i + a < GX) & (j + b >= 0) & (j + b < GY)

    for index, move in enumerate(halo_moves):

        @pl.when(inside(*move[0]))
        def _():
            halo_copy(move, index).start()

    cell = lax.broadcasted_iota(jnp.int32, (8, 128), 0).astype(jnp.float32)
    lane = lax.broadcasted_iota(jnp.int32, (8, 128), 1)
    stacked = [
        jnp.stack([pos_ref[comp, pl.ds(b, 8, stride=8), :] for b in range(8)]) for comp in range(3)
    ]
    charge = jnp.stack([charge_ref[pl.ds(b, 8, stride=8), :] for b in range(8)])
    x = stacked[0] - (2 * i + 1).astype(jnp.float32)
    y = stacked[1] - (2 * j + 1).astype(jnp.float32)
    z = stacked[2] - (2.0 * cell + 1.0)[None]
    moments = zero_tile
    for degree, moment, real, imag in harmonic_columns(x, y, z, ORDER):
        for part, value in enumerate((real, imag)):
            if value is None:
                continue
            summed = jnp.sum(jnp.sum(value * charge, axis=0), axis=1, keepdims=True)
            index = coef_index(degree, moment, part)
            moments = jnp.where(lane == index, scale_of(degree, moment) * summed, moments)
    mg[OWN] = moments.astype(jnp.bfloat16).astype(jnp.float32)

    def multipole_copy(pi, pj):
        there = (i - pi + REACH) * WIDTH + (j - pj + REACH)
        return pltpu.make_async_remote_copy(
            src_ref=mg.at[OWN],
            dst_ref=mg.at[there],
            send_sem=send_m.at[there],
            recv_sem=recv_m.at[there],
            device_id=(pi, pj),
            device_id_type=MESH,
        )

    def send_multipole(t, carry):
        pi, pj, ok = partners(i, j, t)

        @pl.when(ok)
        def _():
            multipole_copy(pi, pj).start()

        return carry

    lax.fori_loop(0, 24, send_multipole, 0)

    def wait_multipole(t, carry):
        pi, pj, ok = partners(i, j, t)

        @pl.when(ok)
        def _():
            multipole_copy(pi, pj).wait_send()
            here = (pi - i + REACH) * WIDTH + (pj - j + REACH)
            pltpu.make_async_remote_copy(
                src_ref=mg.at[OWN],
                dst_ref=mg.at[here],
                send_sem=send_m.at[here],
                recv_sem=recv_m.at[here],
                device_id=(pi, pj),
                device_id_type=MESH,
            ).wait_recv()

        return carry

    lax.fori_loop(0, 24, wait_multipole, 0)
    for index, move in enumerate(halo_moves):
        da, db = move[0]

        @pl.when(inside(da, db))
        def _():
            halo_copy(move, index).wait_send()

        @pl.when(inside(-da, -db))
        def _():
            halo_copy(move, index).wait_recv()

    counts = jnp.zeros((16, 128), jnp.int32)
    lanes = lax.broadcasted_iota(jnp.int32, (16, 128), 1)
    for column in range(16):
        used = jnp.where(tab[column, 3] != 0.0, lanes + 1, 0)
        counts = jnp.where(lanes == column, jnp.max(used, axis=1, keepdims=True), counts)
    cnt[...] = counts


def exchange(pos, charges):
    vmem = pl.BlockSpec(memory_space=pltpu.VMEM)
    return pl.pallas_call(
        exchange_kernel,
        out_shape=(
            jax.ShapeDtypeStruct((16, 4, 16, 128), jnp.float32),
            jax.ShapeDtypeStruct((SLOTS, 8, 128), jnp.float32),
            jax.ShapeDtypeStruct((16, 128), jnp.int32),
        ),
        in_specs=[pl.BlockSpec(memory_space=pltpu.HBM)] * 2,
        out_specs=(vmem, vmem, vmem),
        scratch_shapes=[
            pltpu.VMEM((3, 64, 128), jnp.float32),
            pltpu.VMEM((64, 128), jnp.float32),
            pltpu.SemaphoreType.DMA((2,)),
            pltpu.SemaphoreType.DMA((SLOTS,)),
            pltpu.SemaphoreType.DMA((SLOTS,)),
            pltpu.SemaphoreType.DMA((len(halo_moves),)),
            pltpu.SemaphoreType.DMA((len(halo_moves),)),
        ],
        compiler_params=pltpu.CompilerParams(
            collective_id=0, has_side_effects=True, vmem_limit_bytes=16 << 20
        ),
        name="exchange",
    )(pos, charges)


source_lists = [
    ((5, 6, 9, 10), (5, 6, 9, 10)),
    ((1, 2), (5, 6)),
    ((13, 14), (9, 10)),
    ((4, 8), (5, 9)),
    ((7, 11), (6, 10)),
    ((0,), (5,)),
    ((3,), (6,)),
    ((12,), (9,)),
    ((15,), (10,)),
]
own_columns = (5, 6, 9, 10)
unrolls = {4: 8, 2: 8, 1: 8}
depths = {4: 1, 2: 1, 1: 2}
ring_slots = [4 * 16 * len(sources) for sources, _ in source_lists]
ring_base = [sum(ring_slots[:n]) for n in range(len(ring_slots))]
RING = sum(ring_slots)


def build_sources(cnt, columns, starts, ring, z):
    row = lax.broadcasted_iota(jnp.int32, (256, 512), 0)
    comp_of = lax.broadcasted_iota(jnp.int32, (256, 512), 1) // 128
    pick = ((row % 64 == comp_of * 16 + z) & (row < 192)).astype(jnp.float32).astype(jnp.bfloat16)
    for n, (sources, _) in enumerate(source_lists):
        base = sum(len(s) for s, _ in source_lists[:n]) * 128
        spread = jnp.dot(
            columns[base : base + 128 * len(sources), :], pick, preferred_element_type=jnp.float32
        )
        offset = starts[n, z]
        for k, column in enumerate(sources):
            for g in range(16):
                slot = ring_base[n] + ((offset + g) & (ring_slots[n] - 1))
                rows = slice(128 * k + 8 * g, 128 * k + 8 * g + 8)
                for comp in range(4):
                    ring[slot, comp] = spread[rows, 128 * comp : 128 * comp + 128]
            offset = offset + (cnt[z, column] + 7) // 8
        starts[n, z + 1] = offset


def near_slab(tab, starts, ring, near, z):
    for n, (_, targets) in enumerate(source_lists):
        unroll = unrolls[len(targets)]
        first = starts[n, jnp.maximum(z - 1, 0)]
        last = starts[n, jnp.minimum(z + 2, 16)]
        at = [
            [jnp.broadcast_to(tab[t, comp, pl.ds(z, 1), :], (8, 128)) for comp in range(3)]
            for t in targets
        ]
        if n == 0:
            init = tuple(jnp.zeros((8, 128), jnp.float32) for _ in range(4 * len(targets)))
        else:
            init = tuple(near[comp, t, z] for t in targets for comp in range(4))

        def front(granule):
            slot = ring_base[n] + (jnp.minimum(granule, last - 1) & (ring_slots[n] - 1))
            xs, ys, zs, cs = (ring[slot, comp] for comp in range(4))
            made = [jnp.where(granule < last, cs, 0.0)]
            for x, y, z in at:
                dx, dy, dz = x - xs, y - ys, z - zs
                made += [dx, dy, dz, dx * dx + dy * dy + (dz * dz + SOFTENING)]
            return made

        def body(it, carry):
            sums, queue = list(carry[0]), list(carry[1])
            for u in range(unroll):
                queue.append(front(first + depth + it * unroll + u))
                cs, *parts = queue.pop(0)
                for k in range(len(targets)):
                    dx, dy, dz, square = parts[4 * k : 4 * k + 4]
                    inverse = lax.rsqrt(square)
                    weight = cs * inverse
                    cubed = weight * (inverse * inverse)
                    sums[4 * k] += weight
                    sums[4 * k + 1] += cubed * dx
                    sums[4 * k + 2] += cubed * dy
                    sums[4 * k + 3] += cubed * dz
            return tuple(sums), queue

        depth = depths[len(targets)]
        queue = [front(first + u) for u in range(depth)]
        sums = lax.fori_loop(0, (last - first + unroll - 1) // unroll, body, (init, queue))[0]
        for k, t in enumerate(targets):
            for comp in range(4):
                near[comp, t, z] = sums[4 * k + comp]


def near_field(tab, cnt, columns, starts, ring, near):
    low_lanes = lax.broadcasted_iota(jnp.int32, (128, 128), 1) < 64
    order = [column for sources, _ in source_lists for column in sources]
    for place, column in enumerate(order):
        flat = tab[column].reshape(64, 128)
        value = jnp.transpose(jnp.concatenate([flat, flat], axis=0))
        high = value.astype(jnp.bfloat16).astype(jnp.float32)
        rest = value - high
        middle = rest.astype(jnp.bfloat16).astype(jnp.float32)
        rows = slice(128 * place, 128 * place + 128)
        columns[rows, :128] = jnp.where(low_lanes, high, middle).astype(jnp.bfloat16)
        columns[rows, 128:] = jnp.where(low_lanes, rest - middle, 0.0).astype(jnp.bfloat16)
    for n in range(len(source_lists)):
        starts[n, 0] = 0

    def step(z, carry):
        @pl.when(z < 16)
        def _():
            build_sources(cnt, columns, starts, ring, z)

        @pl.when(z > 0)
        def _():
            near_slab(tab, starts, ring, near, z - 1)

        return carry

    lax.fori_loop(0, 17, step, 0)


def stack_multipoles(mg, padded, stacked):
    cell = lax.broadcasted_iota(jnp.int32, (8, 128), 0)
    lane = lax.broadcasted_iota(jnp.int32, (8, 128), 1)
    padded[...] = jnp.zeros(padded.shape, jnp.float32)
    for s in range(SLOTS):
        padded[s, 8:16, :] = mg[s]
    even = cell % 2 == 0
    current = jnp.zeros((8, 128), jnp.float32)
    for k, (a, b, c) in enumerate(far_offsets):
        value = padded[(a + REACH) * WIDTH + b + REACH, 8 + c : 16 + c, :]
        if c == 3:
            value = jnp.where(even, value, 0.0)
        elif c == -3:
            value = jnp.where(even, 0.0, value)
        tile, shift = divmod(k * COEF, 128)
        rolled = pltpu.roll(value, shift, 1) if shift else value
        current = jnp.where(lane >= shift, rolled, current)
        if shift + COEF >= 128:
            stacked[:, tile * 128 : tile * 128 + 128] = current
            current = rolled
    last = CLASSES * COEF
    tile, shift = divmod(last, 128)
    if shift:
        stacked[:, tile * 128 : tile * 128 + 128] = jnp.where(lane < shift, current, 0.0)


CHUNK = 4096


def local_expansion(stacked, operator):
    total = jnp.zeros((8, COEF), jnp.float32)
    width = CLASSES * COEF
    for start in range(0, width, CHUNK):
        stop = min(start + CHUNK, width)
        total += lax.dot_general(
            stacked[:, start:stop].astype(jnp.bfloat16),
            operator[start:stop, :],
            (((1,), (0,)), ((), ())),
            preferred_element_type=jnp.float32,
        )
    return total


def far_tables(local, coefs):
    def factor(degree, moment):
        if degree > ORDER or moment > degree:
            return None
        scale = scale_of(degree, moment)
        pick = lambda index: jnp.broadcast_to(local[:, index : index + 1], (8, 128)) * scale
        real = pick(coef_index(degree, moment))
        imag = -pick(coef_index(degree, moment, 1)) if moment else None
        return real, imag

    zero = jnp.zeros((8, 128), jnp.float32)
    index = 0
    for moment in range(ORDER + 1):
        for degree in range(moment, ORDER + 1):
            own = factor(degree, moment)
            coefs[0, index, 0] = own[0]
            if moment:
                coefs[0, index, 1] = own[1]
            if degree < ORDER:
                below = factor(degree + 1, moment - 1) if moment else None
                above = factor(degree + 1, moment + 1)
                level = factor(degree + 1, moment)
                weight = 1.0 if moment == 1 else 0.5
                low = (zero, zero)
                if below:
                    low = (weight * below[0], zero if below[1] is None else weight * below[1])
                high = (0.5 * above[0], 0.5 * above[1])
                coefs[1, index, 0] = low[0] - high[0]
                coefs[2, index, 0] = low[1] + high[1]
                coefs[3, index, 0] = level[0]
                if moment:
                    coefs[1, index, 1] = low[1] - high[1]
                    coefs[2, index, 1] = -(low[0] + high[0])
                    coefs[3, index, 1] = level[1]
            index += 1


def finish(tab, near, coefs, pot_ref, field_ref):
    i = lax.axis_index("gx")
    j = lax.axis_index("gy")
    cell = lax.broadcasted_iota(jnp.int32, (8, 128), 0).astype(jnp.float32)
    self_term = lax.rsqrt(jnp.full((8, 128), SOFTENING, jnp.float32))
    for bz in range(2):
        rows = pl.ds(bz, 8, stride=2)
        pick = lambda comp: jnp.stack([tab[t, comp, rows, :] for t in own_columns])
        x = pick(0) - (2 * i + 1).astype(jnp.float32)
        y = pick(1) - (2 * j + 1).astype(jnp.float32)
        z = pick(2) - (2.0 * cell + 1.0)[None]
        sums = [jnp.zeros((4, 8, 128), jnp.float32) for _ in range(4)]
        index = 0
        for degree, moment, real, imag in harmonic_columns(x, y, z, ORDER):
            for out in range(4 if degree < ORDER else 1):
                sums[out] += coefs[out, index, 0][None] * real
                if moment:
                    sums[out] -= coefs[out, index, 1][None] * imag
            index += 1
        for k, t in enumerate(own_columns):
            leaf = (t // 4 - 1) + 2 * (t % 4 - 1) + 4 * bz
            dest = pl.ds(leaf, 8, stride=8)
            pair = [near[comp, t, rows] for comp in range(4)]
            close = [jnp.sum(v, axis=1) for v in pair]
            charge = tab[t, 3, rows, :]
            pot_ref[dest, :] = sums[0][k] + (close[0] - charge * self_term)
            for comp in range(3):
                field_ref[comp, dest, :] = close[comp + 1] - sums[comp + 1][k]


def evaluate_kernel(
    cnt, tab, mg, translations, pot_ref, field_ref,
    columns, starts, ring, near, padded, stacked, operator, coefs, copy_sem,
):
    fetch = pltpu.make_async_copy(translations, operator, copy_sem)
    fetch.start()
    near_field(tab, cnt, columns, starts, ring, near)
    stack_multipoles(mg, padded, stacked)
    fetch.wait()
    local = local_expansion(stacked, operator)
    far_tables(local, coefs)
    finish(tab, near, coefs, pot_ref, field_ref)


def evaluate(cnt, tab, mg, translations):
    vmem = pl.BlockSpec(memory_space=pltpu.VMEM)
    f32 = jnp.float32
    return pl.pallas_call(
        evaluate_kernel,
        out_shape=(
            jax.ShapeDtypeStruct((64, 128), f32),
            jax.ShapeDtypeStruct((3, 64, 128), f32),
        ),
        in_specs=[
            pl.BlockSpec(memory_space=pltpu.SMEM),
            vmem,
            vmem,
            pl.BlockSpec(memory_space=pl.ANY),
        ],
        out_specs=(vmem, vmem),
        scratch_shapes=[
            pltpu.VMEM((2048, 256), jnp.bfloat16),
            pltpu.SMEM((len(source_lists), 17), jnp.int32),
            pltpu.VMEM((RING, 4, 8, 128), f32),
            pltpu.VMEM((4, 16, 16, 8, 128), f32),
            pltpu.VMEM((SLOTS, 24, 128), f32),
            pltpu.VMEM((8, TILES * 128), f32),
            pltpu.VMEM((CLASSES * COEF, COEF), jnp.bfloat16),
            pltpu.VMEM((4, 66, 2, 8, 128), f32),
            pltpu.SemaphoreType.DMA,
        ],
        compiler_params=pltpu.CompilerParams(vmem_limit_bytes=50 << 20),
        name="evaluate",
    )(cnt, tab, mg, translations)


def per_device(
    positions, charges, send_x, send_y, send_corner, near_slot, far_sources, translations
):
    tab, mg, cnt = exchange(jnp.transpose(positions, (1, 0, 2)), charges)
    potential, field = evaluate(cnt, tab, mg, jnp.transpose(translations))
    return potential, jnp.transpose(field, (1, 0, 2))


def solution(mesh):
    return jax.shard_map(
        per_device,
        mesh=mesh,
        in_specs=(
            P(("gx", "gy"), None, None),
            P(("gx", "gy"), None),
            P(("gx", "gy"), None, None),
            P(("gx", "gy"), None, None),
            P(("gx", "gy"), None, None),
            P(("gx", "gy"), None),
            P(("gx", "gy"), None),
            P(),
        ),
        out_specs=(P(("gx", "gy"), None), P(("gx", "gy"), None, None)),
        check_vma=False,
    )
```

```python
import math

import jax
import jax.numpy as jnp
from jax import lax
from jax.experimental import pallas as pl
from jax.experimental.pallas import tpu as pltpu
from jax.sharding import PartitionSpec as P

ORDER = 10
COEF = 121
CLASSES = 316
SOFTENING = 0.01
GX = 4
GY = 32
REACH = 3
WIDTH = 2 * REACH + 1
SLOTS = WIDTH * WIDTH
OWN = SLOTS // 2
TILES = 299
MESH = pl.DeviceIdType.MESH

far_offsets = [
    (a, b, c)
    for a in range(-3, 4)
    for b in range(-3, 4)
    for c in range(-3, 4)
    if max(abs(a), abs(b), abs(c)) > 1
]


def scale_of(degree, moment):
    return math.sqrt(math.factorial(degree + moment) * math.factorial(degree - moment))


def coef_index(degree, moment, imag=0):
    return degree * degree + (2 * moment - 1 + imag if moment else 0)


def harmonic_columns(x, y, z, order):
    radius_sq = x * x + y * y + z * z
    diag = (jnp.ones_like(x), None)
    for moment in range(order + 1):
        if moment == 1:
            diag = (-0.5 * x, -0.5 * y)
        elif moment > 1:
            factor = -0.5 / moment
            real, imag = diag
            diag = (factor * (x * real - y * imag), factor * (x * imag + y * real))
        yield moment, moment, diag[0], diag[1]
        two_back, one_back = None, diag
        for degree in range(moment + 1, order + 1):
            if degree == moment + 1:
                step = tuple(None if v is None else z * v for v in one_back)
            else:
                factor = 1.0 / ((degree - moment) * (degree + moment))
                zf = (factor * (2 * degree - 1)) * z
                rf = factor * radius_sq
                step = tuple(
                    None if v is None else zf * v - rf * w for v, w in zip(one_back, two_back)
                )
            yield degree, moment, step[0], step[1]
            two_back, one_back = one_back, step


def partners(i, j, t):
    pi = t // 6
    pj = (j // 2) * 2 - 2 + t % 6
    ok = (pj >= 0) & (pj < GY) & ((pi != i) | (pj != j))
    return pi, pj, ok


halo_moves = (
    [((1, 0), 9 + y, 1 + y) for y in range(2)]
    + [((-1, 0), 5 + y, 13 + y) for y in range(2)]
    + [((0, 1), 4 * x + 2, 4 * x) for x in (1, 2)]
    + [((0, -1), 4 * x + 1, 4 * x + 3) for x in (1, 2)]
    + [((1, 1), 10, 0), ((1, -1), 9, 3), ((-1, 1), 6, 12), ((-1, -1), 5, 15)]
)


def exchange_kernel(
    pos_any, charge_any, tab, mg, cnt,
    pos_ref, charge_ref, fetch_sem, send_m, recv_m, send_h, recv_h,
):
    i = lax.axis_index("gx")
    j = lax.axis_index("gy")
    zero_tile = jnp.zeros((8, 128), jnp.float32)
    fetches = [
        pltpu.make_async_copy(pos_any, pos_ref, fetch_sem.at[0]),
        pltpu.make_async_copy(charge_any, charge_ref, fetch_sem.at[1]),
    ]
    for fetch in fetches:
        fetch.start()
    mg[...] = jnp.zeros(mg.shape, jnp.float32)
    for column in range(16):
        if column not in (5, 6, 9, 10):
            tab[column] = jnp.zeros(tab.shape[1:], jnp.float32)

    barrier = pltpu.get_barrier_semaphore()

    def signal_partner(t, count):
        pi, pj, ok = partners(i, j, t)

        @pl.when(ok)
        def _():
            pl.semaphore_signal(barrier, inc=1, device_id=(pi, pj), device_id_type=MESH)

        return count + ok.astype(jnp.int32)

    total = lax.fori_loop(0, 24, signal_partner, jnp.int32(0))
    for fetch in fetches:
        fetch.wait()
    for bx in range(2):
        for by in range(2):
            column = 4 * (1 + bx) + 1 + by
            for bz in range(2):
                rows = pl.ds(bx + 2 * by + 4 * bz, 8, stride=8)
                dest = pl.ds(bz, 8, stride=2)
                for comp in range(3):
                    tab[column, comp, dest, :] = pos_ref[comp, rows, :]
                tab[column, 3, dest, :] = charge_ref[rows, :]

    def halo_copy(move, index):
        (da, db), source, dest = move
        return pltpu.make_async_remote_copy(
            src_ref=tab.at[source],
            dst_ref=tab.at[dest],
            send_sem=send_h.at[index],
            recv_sem=recv_h.at[index],
            device_id=(i + da, j + db),
            device_id_type=MESH,
        )

    def inside(a, b):
        return (i + a >= 0) & (i + a < GX) & (j + b >= 0) & (j + b < GY)

    cell = lax.broadcasted_iota(jnp.int32, (8, 128), 0).astype(jnp.float32)
    lane = lax.broadcasted_iota(jnp.int32, (8, 128), 1)
    stacked = [
        jnp.stack([pos_ref[comp, pl.ds(b, 8, stride=8), :] for b in range(8)]) for comp in range(3)
    ]
    charge = jnp.stack([charge_ref[pl.ds(b, 8, stride=8), :] for b in range(8)])
    x = stacked[0] - (2 * i + 1).astype(jnp.float32)
    y = stacked[1] - (2 * j + 1).astype(jnp.float32)
    z = stacked[2] - (2.0 * cell + 1.0)[None]
    moments = zero_tile
    for degree, moment, real, imag in harmonic_columns(x, y, z, ORDER):
        for part, value in enumerate((real, imag)):
            if value is None:
                continue
            summed = jnp.sum(jnp.sum(value * charge, axis=0), axis=1, keepdims=True)
            index = coef_index(degree, moment, part)
            moments = jnp.where(lane == index, scale_of(degree, moment) * summed, moments)
    mg[OWN] = moments.astype(jnp.bfloat16).astype(jnp.float32)
    pl.semaphore_wait(barrier, total)

    def multipole_copy(pi, pj):
        there = (i - pi + REACH) * WIDTH + (j - pj + REACH)
        return pltpu.make_async_remote_copy(
            src_ref=mg.at[OWN],
            dst_ref=mg.at[there],
            send_sem=send_m.at[there],
            recv_sem=recv_m.at[there],
            device_id=(pi, pj),
            device_id_type=MESH,
        )

    def send_multipole(t, carry):
        pi, pj, ok = partners(i, j, t)

        @pl.when(ok)
        def _():
            multipole_copy(pi, pj).start()

        return carry

    lax.fori_loop(0, 24, send_multipole, 0)

    for index, move in enumerate(halo_moves):

        @pl.when(inside(*move[0]))
        def _():
            halo_copy(move, index).start()

    def wait_multipole(t, carry):
        pi, pj, ok = partners(i, j, t)

        @pl.when(ok)
        def _():
            multipole_copy(pi, pj).wait_send()
            here = (pi - i + REACH) * WIDTH + (pj - j + REACH)
            pltpu.make_async_remote_copy(
                src_ref=mg.at[OWN],
                dst_ref=mg.at[here],
                send_sem=send_m.at[here],
                recv_sem=recv_m.at[here],
                device_id=(pi, pj),
                device_id_type=MESH,
            ).wait_recv()

        return carry

    lax.fori_loop(0, 24, wait_multipole, 0)
    for index, move in enumerate(halo_moves):
        da, db = move[0]

        @pl.when(inside(da, db))
        def _():
            halo_copy(move, index).wait_send()

        @pl.when(inside(-da, -db))
        def _():
            halo_copy(move, index).wait_recv()

    counts = jnp.zeros((16, 128), jnp.int32)
    lanes = lax.broadcasted_iota(jnp.int32, (16, 128), 1)
    for column in range(16):
        used = jnp.where(tab[column, 3] != 0.0, lanes + 1, 0)
        counts = jnp.where(lanes == column, jnp.max(used, axis=1, keepdims=True), counts)
    cnt[...] = counts


def exchange(pos, charges):
    vmem = pl.BlockSpec(memory_space=pltpu.VMEM)
    return pl.pallas_call(
        exchange_kernel,
        out_shape=(
            jax.ShapeDtypeStruct((16, 4, 16, 128), jnp.float32),
            jax.ShapeDtypeStruct((SLOTS, 8, 128), jnp.float32),
            jax.ShapeDtypeStruct((16, 128), jnp.int32),
        ),
        in_specs=[pl.BlockSpec(memory_space=pltpu.HBM)] * 2,
        out_specs=(vmem, vmem, vmem),
        scratch_shapes=[
            pltpu.VMEM((3, 64, 128), jnp.float32),
            pltpu.VMEM((64, 128), jnp.float32),
            pltpu.SemaphoreType.DMA((2,)),
            pltpu.SemaphoreType.DMA((SLOTS,)),
            pltpu.SemaphoreType.DMA((SLOTS,)),
            pltpu.SemaphoreType.DMA((len(halo_moves),)),
            pltpu.SemaphoreType.DMA((len(halo_moves),)),
        ],
        compiler_params=pltpu.CompilerParams(
            collective_id=0, has_side_effects=True, vmem_limit_bytes=16 << 20
        ),
        name="exchange",
    )(pos, charges)


source_lists = [
    ((5, 6, 9, 10), (5, 6, 9, 10)),
    ((1, 2), (5, 6)),
    ((13, 14), (9, 10)),
    ((4, 8), (5, 9)),
    ((7, 11), (6, 10)),
    ((0,), (5,)),
    ((3,), (6,)),
    ((12,), (9,)),
    ((15,), (10,)),
]
own_columns = (5, 6, 9, 10)
unrolls = {4: 8, 2: 8, 1: 8}
depths = {4: 1, 2: 1, 1: 2}
ring_slots = [4 * 16 * len(sources) for sources, _ in source_lists]
ring_base = [sum(ring_slots[:n]) for n in range(len(ring_slots))]
RING = sum(ring_slots)


def build_sources(cnt, columns, starts, ring, z):
    row = lax.broadcasted_iota(jnp.int32, (256, 512), 0)
    comp_of = lax.broadcasted_iota(jnp.int32, (256, 512), 1) // 128
    pick = ((row % 64 == comp_of * 16 + z) & (row < 192)).astype(jnp.float32).astype(jnp.bfloat16)
    for n, (sources, _) in enumerate(source_lists):
        base = sum(len(s) for s, _ in source_lists[:n]) * 128
        spread = jnp.dot(
            columns[base : base + 128 * len(sources), :], pick, preferred_element_type=jnp.float32
        )
        offset = starts[n, z]
        for k, column in enumerate(sources):
            for g in range(16):
                slot = ring_base[n] + ((offset + g) & (ring_slots[n] - 1))
                rows = slice(128 * k + 8 * g, 128 * k + 8 * g + 8)
                for comp in range(4):
                    ring[slot, comp] = spread[rows, 128 * comp : 128 * comp + 128]
            offset = offset + (cnt[z, column] + 7) // 8
        starts[n, z + 1] = offset


def near_slab(tab, starts, ring, near, z):
    for n, (_, targets) in enumerate(source_lists):
        unroll = unrolls[len(targets)]
        first = starts[n, jnp.maximum(z - 1, 0)]
        last = starts[n, jnp.minimum(z + 2, 16)]
        at = [
            [jnp.broadcast_to(tab[t, comp, pl.ds(z, 1), :], (8, 128)) for comp in range(3)]
            for t in targets
        ]
        if n == 0:
            init = tuple(jnp.zeros((8, 128), jnp.float32) for _ in range(4 * len(targets)))
        else:
            init = tuple(near[comp, t, z] for t in targets for comp in range(4))

        def front(granule):
            slot = ring_base[n] + (jnp.minimum(granule, last - 1) & (ring_slots[n] - 1))
            xs, ys, zs, cs = (ring[slot, comp] for comp in range(4))
            made = [jnp.where(granule < last, cs, 0.0)]
            for x, y, z in at:
                dx, dy, dz = x - xs, y - ys, z - zs
                made += [dx, dy, dz, dx * dx + dy * dy + (dz * dz + SOFTENING)]
            return made

        def body(it, carry):
            sums, queue = list(carry[0]), list(carry[1])
            for u in range(unroll):
                queue.append(front(first + depth + it * unroll + u))
                cs, *parts = queue.pop(0)
                for k in range(len(targets)):
                    dx, dy, dz, square = parts[4 * k : 4 * k + 4]
                    inverse = lax.rsqrt(square)
                    weight = cs * inverse
                    cubed = weight * (inverse * inverse)
                    sums[4 * k] += weight
                    sums[4 * k + 1] += cubed * dx
                    sums[4 * k + 2] += cubed * dy
                    sums[4 * k + 3] += cubed * dz
            return tuple(sums), queue

        depth = depths[len(targets)]
        queue = [front(first + u) for u in range(depth)]
        sums = lax.fori_loop(0, (last - first + unroll - 1) // unroll, body, (init, queue))[0]
        for k, t in enumerate(targets):
            for comp in range(4):
                near[comp, t, z] = sums[4 * k + comp]


def near_field(tab, cnt, columns, starts, ring, near):
    low_lanes = lax.broadcasted_iota(jnp.int32, (128, 128), 1) < 64
    order = [column for sources, _ in source_lists for column in sources]
    for place, column in enumerate(order):
        flat = tab[column].reshape(64, 128)
        value = jnp.transpose(jnp.concatenate([flat, flat], axis=0))
        high = value.astype(jnp.bfloat16).astype(jnp.float32)
        rest = value - high
        middle = rest.astype(jnp.bfloat16).astype(jnp.float32)
        rows = slice(128 * place, 128 * place + 128)
        columns[rows, :128] = jnp.where(low_lanes, high, middle).astype(jnp.bfloat16)
        columns[rows, 128:] = jnp.where(low_lanes, rest - middle, 0.0).astype(jnp.bfloat16)
    for n in range(len(source_lists)):
        starts[n, 0] = 0

    def step(z, carry):
        @pl.when(z < 16)
        def _():
            build_sources(cnt, columns, starts, ring, z)

        @pl.when(z > 0)
        def _():
            near_slab(tab, starts, ring, near, z - 1)

        return carry

    lax.fori_loop(0, 17, step, 0)


def stack_multipoles(mg, padded, stacked):
    cell = lax.broadcasted_iota(jnp.int32, (8, 128), 0)
    lane = lax.broadcasted_iota(jnp.int32, (8, 128), 1)
    padded[...] = jnp.zeros(padded.shape, jnp.float32)
    for s in range(SLOTS):
        padded[s, 8:16, :] = mg[s]
    even = cell % 2 == 0
    current = jnp.zeros((8, 128), jnp.float32)
    for k, (a, b, c) in enumerate(far_offsets):
        value = padded[(a + REACH) * WIDTH + b + REACH, 8 + c : 16 + c, :]
        if c == 3:
            value = jnp.where(even, value, 0.0)
        elif c == -3:
            value = jnp.where(even, 0.0, value)
        tile, shift = divmod(k * COEF, 128)
        rolled = pltpu.roll(value, shift, 1) if shift else value
        current = jnp.where(lane >= shift, rolled, current)
        if shift + COEF >= 128:
            stacked[:, tile * 128 : tile * 128 + 128] = current
            current = rolled
    last = CLASSES * COEF
    tile, shift = divmod(last, 128)
    if shift:
        stacked[:, tile * 128 : tile * 128 + 128] = jnp.where(lane < shift, current, 0.0)


CHUNK = 4096


def local_expansion(stacked, operator):
    total = jnp.zeros((8, COEF), jnp.float32)
    width = CLASSES * COEF
    for start in range(0, width, CHUNK):
        stop = min(start + CHUNK, width)
        total += lax.dot_general(
            stacked[:, start:stop].astype(jnp.bfloat16),
            operator[start:stop, :],
            (((1,), (0,)), ((), ())),
            preferred_element_type=jnp.float32,
        )
    return total


def far_tables(local, coefs):
    def factor(degree, moment):
        if degree > ORDER or moment > degree:
            return None
        scale = scale_of(degree, moment)
        pick = lambda index: jnp.broadcast_to(local[:, index : index + 1], (8, 128)) * scale
        real = pick(coef_index(degree, moment))
        imag = -pick(coef_index(degree, moment, 1)) if moment else None
        return real, imag

    zero = jnp.zeros((8, 128), jnp.float32)
    index = 0
    for moment in range(ORDER + 1):
        for degree in range(moment, ORDER + 1):
            own = factor(degree, moment)
            coefs[0, index, 0] = own[0]
            if moment:
                coefs[0, index, 1] = own[1]
            if degree < ORDER:
                below = factor(degree + 1, moment - 1) if moment else None
                above = factor(degree + 1, moment + 1)
                level = factor(degree + 1, moment)
                weight = 1.0 if moment == 1 else 0.5
                low = (zero, zero)
                if below:
                    low = (weight * below[0], zero if below[1] is None else weight * below[1])
                high = (0.5 * above[0], 0.5 * above[1])
                coefs[1, index, 0] = low[0] - high[0]
                coefs[2, index, 0] = low[1] + high[1]
                coefs[3, index, 0] = level[0]
                if moment:
                    coefs[1, index, 1] = low[1] - high[1]
                    coefs[2, index, 1] = -(low[0] + high[0])
                    coefs[3, index, 1] = level[1]
            index += 1


def finish(tab, near, coefs, pot_ref, field_ref):
    i = lax.axis_index("gx")
    j = lax.axis_index("gy")
    cell = lax.broadcasted_iota(jnp.int32, (8, 128), 0).astype(jnp.float32)
    self_term = lax.rsqrt(jnp.full((8, 128), SOFTENING, jnp.float32))
    for bz in range(2):
        rows = pl.ds(bz, 8, stride=2)
        pick = lambda comp: jnp.stack([tab[t, comp, rows, :] for t in own_columns])
        x = pick(0) - (2 * i + 1).astype(jnp.float32)
        y = pick(1) - (2 * j + 1).astype(jnp.float32)
        z = pick(2) - (2.0 * cell + 1.0)[None]
        sums = [jnp.zeros((4, 8, 128), jnp.float32) for _ in range(4)]
        index = 0
        for degree, moment, real, imag in harmonic_columns(x, y, z, ORDER):
            for out in range(4 if degree < ORDER else 1):
                sums[out] += coefs[out, index, 0][None] * real
                if moment:
                    sums[out] -= coefs[out, index, 1][None] * imag
            index += 1
        for k, t in enumerate(own_columns):
            leaf = (t // 4 - 1) + 2 * (t % 4 - 1) + 4 * bz
            dest = pl.ds(leaf, 8, stride=8)
            pair = [near[comp, t, rows] for comp in range(4)]
            close = [jnp.sum(v, axis=1) for v in pair]
            charge = tab[t, 3, rows, :]
            pot_ref[dest, :] = sums[0][k] + (close[0] - charge * self_term)
            for comp in range(3):
                field_ref[comp, dest, :] = close[comp + 1] - sums[comp + 1][k]


def evaluate_kernel(
    cnt, tab, mg, translations, pot_ref, field_ref,
    columns, starts, ring, near, padded, stacked, operator, coefs, copy_sem,
):
    fetch = pltpu.make_async_copy(translations, operator, copy_sem)
    fetch.start()
    near_field(tab, cnt, columns, starts, ring, near)
    stack_multipoles(mg, padded, stacked)
    fetch.wait()
    local = local_expansion(stacked, operator)
    far_tables(local, coefs)
    finish(tab, near, coefs, pot_ref, field_ref)


def evaluate(cnt, tab, mg, translations):
    vmem = pl.BlockSpec(memory_space=pltpu.VMEM)
    f32 = jnp.float32
    return pl.pallas_call(
        evaluate_kernel,
        out_shape=(
            jax.ShapeDtypeStruct((64, 128), f32),
            jax.ShapeDtypeStruct((3, 64, 128), f32),
        ),
        in_specs=[
            pl.BlockSpec(memory_space=pltpu.SMEM),
            vmem,
            vmem,
            pl.BlockSpec(memory_space=pl.ANY),
        ],
        out_specs=(vmem, vmem),
        scratch_shapes=[
            pltpu.VMEM((2048, 256), jnp.bfloat16),
            pltpu.SMEM((len(source_lists), 17), jnp.int32),
            pltpu.VMEM((RING, 4, 8, 128), f32),
            pltpu.VMEM((4, 16, 16, 8, 128), f32),
            pltpu.VMEM((SLOTS, 24, 128), f32),
            pltpu.VMEM((8, TILES * 128), f32),
            pltpu.VMEM((CLASSES * COEF, COEF), jnp.bfloat16),
            pltpu.VMEM((4, 66, 2, 8, 128), f32),
            pltpu.SemaphoreType.DMA,
        ],
        compiler_params=pltpu.CompilerParams(vmem_limit_bytes=50 << 20),
        name="evaluate",
    )(cnt, tab, mg, translations)


def per_device(
    positions, charges, send_x, send_y, send_corner, near_slot, far_sources, translations
):
    tab, mg, cnt = exchange(jnp.transpose(positions, (1, 0, 2)), charges)
    potential, field = evaluate(cnt, tab, mg, jnp.transpose(translations))
    return potential, jnp.transpose(field, (1, 0, 2))


def solution(mesh):
    return jax.shard_map(
        per_device,
        mesh=mesh,
        in_specs=(
            P(("gx", "gy"), None, None),
            P(("gx", "gy"), None),
            P(("gx", "gy"), None, None),
            P(("gx", "gy"), None, None),
            P(("gx", "gy"), None, None),
            P(("gx", "gy"), None),
            P(("gx", "gy"), None),
            P(),
        ),
        out_specs=(P(("gx", "gy"), None), P(("gx", "gy"), None, None)),
        check_vma=False,
    )
```

```python
import math

import jax
import jax.numpy as jnp
from jax import lax
from jax.experimental import pallas as pl
from jax.experimental.pallas import tpu as pltpu
from jax.sharding import PartitionSpec as P

ORDER = 10
COEF = 121
CLASSES = 316
SOFTENING = 0.01
GX = 4
GY = 32
REACH = 3
WIDTH = 2 * REACH + 1
SLOTS = WIDTH * WIDTH
OWN = SLOTS // 2
TILES = 299
MESH = pl.DeviceIdType.MESH

far_offsets = [
    (a, b, c)
    for a in range(-3, 4)
    for b in range(-3, 4)
    for c in range(-3, 4)
    if max(abs(a), abs(b), abs(c)) > 1
]


def scale_of(degree, moment):
    return math.sqrt(math.factorial(degree + moment) * math.factorial(degree - moment))


def coef_index(degree, moment, imag=0):
    return degree * degree + (2 * moment - 1 + imag if moment else 0)


def harmonic_columns(x, y, z, order):
    radius_sq = x * x + y * y + z * z
    diag = (jnp.ones_like(x), None)
    for moment in range(order + 1):
        if moment == 1:
            diag = (-0.5 * x, -0.5 * y)
        elif moment > 1:
            factor = -0.5 / moment
            real, imag = diag
            diag = (factor * (x * real - y * imag), factor * (x * imag + y * real))
        yield moment, moment, diag[0], diag[1]
        two_back, one_back = None, diag
        for degree in range(moment + 1, order + 1):
            if degree == moment + 1:
                step = tuple(None if v is None else z * v for v in one_back)
            else:
                factor = 1.0 / ((degree - moment) * (degree + moment))
                zf = (factor * (2 * degree - 1)) * z
                rf = factor * radius_sq
                step = tuple(
                    None if v is None else zf * v - rf * w for v, w in zip(one_back, two_back)
                )
            yield degree, moment, step[0], step[1]
            two_back, one_back = one_back, step


def partners(i, j, t):
    pi = t // 6
    pj = (j // 2) * 2 - 2 + t % 6
    ok = (pj >= 0) & (pj < GY) & ((pi != i) | (pj != j))
    return pi, pj, ok


halo_moves = (
    [((1, 0), 9 + y, 1 + y) for y in range(2)]
    + [((-1, 0), 5 + y, 13 + y) for y in range(2)]
    + [((0, 1), 4 * x + 2, 4 * x) for x in (1, 2)]
    + [((0, -1), 4 * x + 1, 4 * x + 3) for x in (1, 2)]
    + [((1, 1), 10, 0), ((1, -1), 9, 3), ((-1, 1), 6, 12), ((-1, -1), 5, 15)]
)


def exchange_kernel(
    pos_any, charge_any, tab, mg, cnt,
    pos_ref, charge_ref, fetch_sem, send_m, recv_m, send_h, recv_h,
):
    i = lax.axis_index("gx")
    j = lax.axis_index("gy")
    zero_tile = jnp.zeros((8, 128), jnp.float32)
    fetches = [
        pltpu.make_async_copy(pos_any, pos_ref, fetch_sem.at[0]),
        pltpu.make_async_copy(charge_any, charge_ref, fetch_sem.at[1]),
    ]
    for fetch in fetches:
        fetch.start()
    mg[...] = jnp.zeros(mg.shape, jnp.float32)
    for column in range(16):
        if column not in (5, 6, 9, 10):
            tab[column] = jnp.zeros(tab.shape[1:], jnp.float32)

    barrier = pltpu.get_barrier_semaphore()

    def signal_partner(t, count):
        pi, pj, ok = partners(i, j, t)

        @pl.when(ok)
        def _():
            pl.semaphore_signal(barrier, inc=1, device_id=(pi, pj), device_id_type=MESH)

        return count + ok.astype(jnp.int32)

    total = lax.fori_loop(0, 24, signal_partner, jnp.int32(0))
    for fetch in fetches:
        fetch.wait()
    for bx in range(2):
        for by in range(2):
            column = 4 * (1 + bx) + 1 + by
            for bz in range(2):
                rows = pl.ds(bx + 2 * by + 4 * bz, 8, stride=8)
                dest = pl.ds(bz, 8, stride=2)
                for comp in range(3):
                    tab[column, comp, dest, :] = pos_ref[comp, rows, :]
                tab[column, 3, dest, :] = charge_ref[rows, :]

    def halo_copy(move, index):
        (da, db), source, dest = move
        return pltpu.make_async_remote_copy(
            src_ref=tab.at[source],
            dst_ref=tab.at[dest],
            send_sem=send_h.at[index],
            recv_sem=recv_h.at[index],
            device_id=(i + da, j + db),
            device_id_type=MESH,
        )

    def inside(a, b):
        return (i + a >= 0) & (i + a < GX) & (j + b >= 0) & (j + b < GY)

    cell = lax.broadcasted_iota(jnp.int32, (8, 128), 0).astype(jnp.float32)
    lane = lax.broadcasted_iota(jnp.int32, (8, 128), 1)
    stacked = [
        jnp.stack([pos_ref[comp, pl.ds(b, 8, stride=8), :] for b in range(8)]) for comp in range(3)
    ]
    charge = jnp.stack([charge_ref[pl.ds(b, 8, stride=8), :] for b in range(8)])
    x = stacked[0] - (2 * i + 1).astype(jnp.float32)
    y = stacked[1] - (2 * j + 1).astype(jnp.float32)
    z = stacked[2] - (2.0 * cell + 1.0)[None]
    moments = zero_tile
    for degree, moment, real, imag in harmonic_columns(x, y, z, ORDER):
        for part, value in enumerate((real, imag)):
            if value is None:
                continue
            summed = jnp.sum(jnp.sum(value * charge, axis=0), axis=1, keepdims=True)
            index = coef_index(degree, moment, part)
            moments = jnp.where(lane == index, scale_of(degree, moment) * summed, moments)
    mg[OWN] = moments.astype(jnp.bfloat16).astype(jnp.float32)
    pl.semaphore_wait(barrier, total)

    def multipole_copy(pi, pj):
        there = (i - pi + REACH) * WIDTH + (j - pj + REACH)
        return pltpu.make_async_remote_copy(
            src_ref=mg.at[OWN],
            dst_ref=mg.at[there],
            send_sem=send_m.at[there],
            recv_sem=recv_m.at[there],
            device_id=(pi, pj),
            device_id_type=MESH,
        )

    def send_multipole(t, carry):
        pi, pj, ok = partners(i, j, t)

        @pl.when(ok)
        def _():
            multipole_copy(pi, pj).start()

        return carry

    lax.fori_loop(0, 24, send_multipole, 0)

    for index, move in enumerate(halo_moves):

        @pl.when(inside(*move[0]))
        def _():
            halo_copy(move, index).start()

    def wait_multipole(t, carry):
        pi, pj, ok = partners(i, j, t)

        @pl.when(ok)
        def _():
            multipole_copy(pi, pj).wait_send()
            here = (pi - i + REACH) * WIDTH + (pj - j + REACH)
            pltpu.make_async_remote_copy(
                src_ref=mg.at[OWN],
                dst_ref=mg.at[here],
                send_sem=send_m.at[here],
                recv_sem=recv_m.at[here],
                device_id=(pi, pj),
                device_id_type=MESH,
            ).wait_recv()

        return carry

    lanes = lax.broadcasted_iota(jnp.int32, (16, 128), 1)

    def count_columns(columns, counts):
        for column in columns:
            used = jnp.where(tab[column, 3] != 0.0, lanes + 1, 0)
            counts = jnp.where(lanes == column, jnp.max(used, axis=1, keepdims=True), counts)
        return counts

    own = (5, 6, 9, 10)
    counts = count_columns(own, jnp.zeros((16, 128), jnp.int32))
    lax.fori_loop(0, 24, wait_multipole, 0)
    for index, move in enumerate(halo_moves):
        da, db = move[0]

        @pl.when(inside(da, db))
        def _():
            halo_copy(move, index).wait_send()

        @pl.when(inside(-da, -db))
        def _():
            halo_copy(move, index).wait_recv()

    counts = count_columns([c for c in range(16) if c not in own], counts)
    cnt[...] = counts


def exchange(pos, charges):
    vmem = pl.BlockSpec(memory_space=pltpu.VMEM)
    return pl.pallas_call(
        exchange_kernel,
        out_shape=(
            jax.ShapeDtypeStruct((16, 4, 16, 128), jnp.float32),
            jax.ShapeDtypeStruct((SLOTS, 8, 128), jnp.float32),
            jax.ShapeDtypeStruct((16, 128), jnp.int32),
        ),
        in_specs=[pl.BlockSpec(memory_space=pltpu.HBM)] * 2,
        out_specs=(vmem, vmem, vmem),
        scratch_shapes=[
            pltpu.VMEM((3, 64, 128), jnp.float32),
            pltpu.VMEM((64, 128), jnp.float32),
            pltpu.SemaphoreType.DMA((2,)),
            pltpu.SemaphoreType.DMA((SLOTS,)),
            pltpu.SemaphoreType.DMA((SLOTS,)),
            pltpu.SemaphoreType.DMA((len(halo_moves),)),
            pltpu.SemaphoreType.DMA((len(halo_moves),)),
        ],
        compiler_params=pltpu.CompilerParams(
            collective_id=0, has_side_effects=True, vmem_limit_bytes=16 << 20
        ),
        name="exchange",
    )(pos, charges)


source_lists = [
    ((5, 6, 9, 10), (5, 6, 9, 10)),
    ((1, 2), (5, 6)),
    ((13, 14), (9, 10)),
    ((4, 8), (5, 9)),
    ((7, 11), (6, 10)),
    ((0,), (5,)),
    ((3,), (6,)),
    ((12,), (9,)),
    ((15,), (10,)),
]
own_columns = (5, 6, 9, 10)
unrolls = {4: 8, 2: 8, 1: 8}
depths = {4: 1, 2: 1, 1: 2}
ring_slots = [4 * 16 * len(sources) for sources, _ in source_lists]
ring_base = [sum(ring_slots[:n]) for n in range(len(ring_slots))]
RING = sum(ring_slots)


def build_sources(cnt, columns, starts, ring, z):
    row = lax.broadcasted_iota(jnp.int32, (256, 512), 0)
    comp_of = lax.broadcasted_iota(jnp.int32, (256, 512), 1) // 128
    pick = ((row % 64 == comp_of * 16 + z) & (row < 192)).astype(jnp.float32).astype(jnp.bfloat16)
    for n, (sources, _) in enumerate(source_lists):
        base = sum(len(s) for s, _ in source_lists[:n]) * 128
        spread = jnp.dot(
            columns[base : base + 128 * len(sources), :], pick, preferred_element_type=jnp.float32
        )
        offset = starts[n, z]
        for k, column in enumerate(sources):
            for g in range(16):
                slot = ring_base[n] + ((offset + g) & (ring_slots[n] - 1))
                rows = slice(128 * k + 8 * g, 128 * k + 8 * g + 8)
                for comp in range(4):
                    ring[slot, comp] = spread[rows, 128 * comp : 128 * comp + 128]
            offset = offset + (cnt[z, column] + 7) // 8
        starts[n, z + 1] = offset


def near_slab(tab, starts, ring, near, z):
    for n, (_, targets) in enumerate(source_lists):
        unroll = unrolls[len(targets)]
        first = starts[n, jnp.maximum(z - 1, 0)]
        last = starts[n, jnp.minimum(z + 2, 16)]
        at = [
            [jnp.broadcast_to(tab[t, comp, pl.ds(z, 1), :], (8, 128)) for comp in range(3)]
            for t in targets
        ]
        if n == 0:
            init = tuple(jnp.zeros((8, 128), jnp.float32) for _ in range(4 * len(targets)))
        else:
            init = tuple(near[comp, t, z] for t in targets for comp in range(4))

        def front(granule):
            slot = ring_base[n] + (jnp.minimum(granule, last - 1) & (ring_slots[n] - 1))
            xs, ys, zs, cs = (ring[slot, comp] for comp in range(4))
            made = [jnp.where(granule < last, cs, 0.0)]
            for x, y, z in at:
                dx, dy, dz = x - xs, y - ys, z - zs
                made += [dx, dy, dz, dx * dx + dy * dy + (dz * dz + SOFTENING)]
            return made

        def body(it, carry):
            sums, queue = list(carry[0]), list(carry[1])
            for u in range(unroll):
                queue.append(front(first + depth + it * unroll + u))
                cs, *parts = queue.pop(0)
                for k in range(len(targets)):
                    dx, dy, dz, square = parts[4 * k : 4 * k + 4]
                    inverse = lax.rsqrt(square)
                    weight = cs * inverse
                    cubed = weight * (inverse * inverse)
                    sums[4 * k] += weight
                    sums[4 * k + 1] += cubed * dx
                    sums[4 * k + 2] += cubed * dy
                    sums[4 * k + 3] += cubed * dz
            return tuple(sums), queue

        depth = depths[len(targets)]
        queue = [front(first + u) for u in range(depth)]
        sums = lax.fori_loop(0, (last - first + unroll - 1) // unroll, body, (init, queue))[0]
        for k, t in enumerate(targets):
            for comp in range(4):
                near[comp, t, z] = sums[4 * k + comp]


def near_field(tab, cnt, columns, starts, ring, near):
    low_lanes = lax.broadcasted_iota(jnp.int32, (128, 128), 1) < 64
    order = [column for sources, _ in source_lists for column in sources]
    for place, column in enumerate(order):
        flat = tab[column].reshape(64, 128)
        value = jnp.transpose(jnp.concatenate([flat, flat], axis=0))
        high = value.astype(jnp.bfloat16).astype(jnp.float32)
        rest = value - high
        middle = rest.astype(jnp.bfloat16).astype(jnp.float32)
        rows = slice(128 * place, 128 * place + 128)
        columns[rows, :128] = jnp.where(low_lanes, high, middle).astype(jnp.bfloat16)
        columns[rows, 128:] = jnp.where(low_lanes, rest - middle, 0.0).astype(jnp.bfloat16)
    for n in range(len(source_lists)):
        starts[n, 0] = 0

    def step(z, carry):
        @pl.when(z < 16)
        def _():
            build_sources(cnt, columns, starts, ring, z)

        @pl.when(z > 0)
        def _():
            near_slab(tab, starts, ring, near, z - 1)

        return carry

    lax.fori_loop(0, 17, step, 0)


def stack_multipoles(mg, padded, stacked):
    cell = lax.broadcasted_iota(jnp.int32, (8, 128), 0)
    lane = lax.broadcasted_iota(jnp.int32, (8, 128), 1)
    padded[...] = jnp.zeros(padded.shape, jnp.float32)
    for s in range(SLOTS):
        padded[s, 8:16, :] = mg[s]
    even = cell % 2 == 0
    current = jnp.zeros((8, 128), jnp.float32)
    for k, (a, b, c) in enumerate(far_offsets):
        value = padded[(a + REACH) * WIDTH + b + REACH, 8 + c : 16 + c, :]
        if c == 3:
            value = jnp.where(even, value, 0.0)
        elif c == -3:
            value = jnp.where(even, 0.0, value)
        tile, shift = divmod(k * COEF, 128)
        rolled = pltpu.roll(value, shift, 1) if shift else value
        current = jnp.where(lane >= shift, rolled, current)
        if shift + COEF >= 128:
            stacked[:, tile * 128 : tile * 128 + 128] = current
            current = rolled
    last = CLASSES * COEF
    tile, shift = divmod(last, 128)
    if shift:
        stacked[:, tile * 128 : tile * 128 + 128] = jnp.where(lane < shift, current, 0.0)


CHUNK = 4096


def local_expansion(stacked, operator):
    total = jnp.zeros((8, COEF), jnp.float32)
    width = CLASSES * COEF
    for start in range(0, width, CHUNK):
        stop = min(start + CHUNK, width)
        total += lax.dot_general(
            stacked[:, start:stop].astype(jnp.bfloat16),
            operator[start:stop, :],
            (((1,), (0,)), ((), ())),
            preferred_element_type=jnp.float32,
        )
    return total


def far_tables(local, coefs):
    def factor(degree, moment):
        if degree > ORDER or moment > degree:
            return None
        scale = scale_of(degree, moment)
        pick = lambda index: jnp.broadcast_to(local[:, index : index + 1], (8, 128)) * scale
        real = pick(coef_index(degree, moment))
        imag = -pick(coef_index(degree, moment, 1)) if moment else None
        return real, imag

    zero = jnp.zeros((8, 128), jnp.float32)
    index = 0
    for moment in range(ORDER + 1):
        for degree in range(moment, ORDER + 1):
            own = factor(degree, moment)
            coefs[0, index, 0] = own[0]
            if moment:
                coefs[0, index, 1] = own[1]
            if degree < ORDER:
                below = factor(degree + 1, moment - 1) if moment else None
                above = factor(degree + 1, moment + 1)
                level = factor(degree + 1, moment)
                weight = 1.0 if moment == 1 else 0.5
                low = (zero, zero)
                if below:
                    low = (weight * below[0], zero if below[1] is None else weight * below[1])
                high = (0.5 * above[0], 0.5 * above[1])
                coefs[1, index, 0] = low[0] - high[0]
                coefs[2, index, 0] = low[1] + high[1]
                coefs[3, index, 0] = level[0]
                if moment:
                    coefs[1, index, 1] = low[1] - high[1]
                    coefs[2, index, 1] = -(low[0] + high[0])
                    coefs[3, index, 1] = level[1]
            index += 1


def finish(tab, near, coefs, pot_ref, field_ref):
    i = lax.axis_index("gx")
    j = lax.axis_index("gy")
    cell = lax.broadcasted_iota(jnp.int32, (8, 128), 0).astype(jnp.float32)
    self_term = lax.rsqrt(jnp.full((8, 128), SOFTENING, jnp.float32))
    for bz in range(2):
        rows = pl.ds(bz, 8, stride=2)
        pick = lambda comp: jnp.stack([tab[t, comp, rows, :] for t in own_columns])
        x = pick(0) - (2 * i + 1).astype(jnp.float32)
        y = pick(1) - (2 * j + 1).astype(jnp.float32)
        z = pick(2) - (2.0 * cell + 1.0)[None]
        sums = [jnp.zeros((4, 8, 128), jnp.float32) for _ in range(4)]
        index = 0
        for degree, moment, real, imag in harmonic_columns(x, y, z, ORDER):
            for out in range(4 if degree < ORDER else 1):
                sums[out] += coefs[out, index, 0][None] * real
                if moment:
                    sums[out] -= coefs[out, index, 1][None] * imag
            index += 1
        for k, t in enumerate(own_columns):
            leaf = (t // 4 - 1) + 2 * (t % 4 - 1) + 4 * bz
            dest = pl.ds(leaf, 8, stride=8)
            pair = [near[comp, t, rows] for comp in range(4)]
            close = [jnp.sum(v, axis=1) for v in pair]
            charge = tab[t, 3, rows, :]
            pot_ref[dest, :] = sums[0][k] + (close[0] - charge * self_term)
            for comp in range(3):
                field_ref[comp, dest, :] = close[comp + 1] - sums[comp + 1][k]


def evaluate_kernel(
    cnt, tab, mg, translations, pot_ref, field_ref,
    columns, starts, ring, near, padded, stacked, operator, coefs, copy_sem,
):
    fetch = pltpu.make_async_copy(translations, operator, copy_sem)
    fetch.start()
    near_field(tab, cnt, columns, starts, ring, near)
    stack_multipoles(mg, padded, stacked)
    fetch.wait()
    local = local_expansion(stacked, operator)
    far_tables(local, coefs)
    finish(tab, near, coefs, pot_ref, field_ref)


def evaluate(cnt, tab, mg, translations):
    vmem = pl.BlockSpec(memory_space=pltpu.VMEM)
    f32 = jnp.float32
    return pl.pallas_call(
        evaluate_kernel,
        out_shape=(
            jax.ShapeDtypeStruct((64, 128), f32),
            jax.ShapeDtypeStruct((3, 64, 128), f32),
        ),
        in_specs=[
            pl.BlockSpec(memory_space=pltpu.SMEM),
            vmem,
            vmem,
            pl.BlockSpec(memory_space=pl.ANY),
        ],
        out_specs=(vmem, vmem),
        scratch_shapes=[
            pltpu.VMEM((2048, 256), jnp.bfloat16),
            pltpu.SMEM((len(source_lists), 17), jnp.int32),
            pltpu.VMEM((RING, 4, 8, 128), f32),
            pltpu.VMEM((4, 16, 16, 8, 128), f32),
            pltpu.VMEM((SLOTS, 24, 128), f32),
            pltpu.VMEM((8, TILES * 128), f32),
            pltpu.VMEM((CLASSES * COEF, COEF), jnp.bfloat16),
            pltpu.VMEM((4, 66, 2, 8, 128), f32),
            pltpu.SemaphoreType.DMA,
        ],
        compiler_params=pltpu.CompilerParams(vmem_limit_bytes=50 << 20),
        name="evaluate",
    )(cnt, tab, mg, translations)


def per_device(
    positions, charges, send_x, send_y, send_corner, near_slot, far_sources, translations
):
    tab, mg, cnt = exchange(jnp.transpose(positions, (1, 0, 2)), charges)
    potential, field = evaluate(cnt, tab, mg, jnp.transpose(translations))
    return potential, jnp.transpose(field, (1, 0, 2))


def solution(mesh):
    return jax.shard_map(
        per_device,
        mesh=mesh,
        in_specs=(
            P(("gx", "gy"), None, None),
            P(("gx", "gy"), None),
            P(("gx", "gy"), None, None),
            P(("gx", "gy"), None, None),
            P(("gx", "gy"), None, None),
            P(("gx", "gy"), None),
            P(("gx", "gy"), None),
            P(),
        ),
        out_specs=(P(("gx", "gy"), None), P(("gx", "gy"), None, None)),
        check_vma=False,
    )
```
